256 devices in a mesh: dp: 4 (over y_lo, core), mp: 64 (over x, y_hi, z).
Axes of the slice: x: 4, y: 4 (y_hi: 2, y_lo: 2; y = y_hi * 2 + y_lo), z: 8, core: 2. Of those that a mesh axis runs over, the one named last changes fastest.
Arguments:
- queries: bfloat16 [12288, 256], P('mp'), may hold values from -6 to 6
- keys: bfloat16 [4, 4096, 4096], P('dp', 'mp'), may hold values from -6 to 6
- values: bfloat16 [4, 4096, 4096], P('dp', 'mp'), may hold values from -5.5 to 5.5
- out_cotangent: bfloat16 [4, 12288, 256], P('dp', 'mp'), may hold values from -356.20202 to 356.20202
Outputs:
- query_gradient: float32 [12288, 256], P('mp')
- key_gradient: bfloat16 [4, 4096, 4096], P('dp', 'mp')
- value_gradient: bfloat16 [4, 4096, 4096], P('dp', 'mp')
The draws below stay inside these ranges and needn't reach their ends.
All inputs are finite; a program needn't handle non-finite values.
Results may differ from the reference program's by a relative error of at most 0.02.
Values may be sent and summed in bfloat16 or wider, within the bound.
A program may use at most 64 MiB of HBM per device.

```python
import math
import jax
import jax.numpy as jnp
from jax import lax

HEADS = 16
DH = 256
R = 768
KEYS = 4096
DOCS = 4


def draw_queries(key, part):
    key = jax.random.fold_in(key, 1)
    sample = jnp.clip(jax.random.normal(key, (HEADS * R, DH)), -4.0, 4.0)
    return sample.astype(jnp.bfloat16)


def draw_keys(key, part):
    key = jax.random.fold_in(key, 2)
    sample = jnp.clip(jax.random.normal(key, (DOCS, KEYS, HEADS, DH)), -4.0, 4.0)
    return sample.reshape(DOCS, KEYS, HEADS * DH).astype(jnp.bfloat16)


def draw_values(key, part):
    key = jax.random.fold_in(key, 3)
    column_mean = jax.random.uniform(jax.random.fold_in(key, 7), (DOCS, 1, HEADS * DH), minval=-1.5, maxval=1.5)
    spread = jnp.clip(jax.random.normal(key, (DOCS, KEYS, HEADS * DH)), -4.0, 4.0)
    return (spread + column_mean).astype(jnp.bfloat16)


def draw_out_cotangent(key, part):
    key = jax.random.fold_in(key, 4)
    cotangent_scale = 0.6 * KEYS / math.sqrt(R)
    sample = jnp.clip(jax.random.normal(key, (DOCS, HEADS * R, DH)), -4.0, 4.0) * cotangent_scale
    return sample.astype(jnp.bfloat16)


def setup_inputs(seed: int = 0) -> dict:
    splits = jax.random.split(jax.random.key(seed), 5)
    return {
        "queries": draw_queries(jax.random.fold_in(splits[4], 71), 0),
        "keys": draw_keys(jax.random.fold_in(splits[4], 71), 0),
        "values": draw_values(jax.random.fold_in(splits[4], 71), 0),
        "out_cotangent": draw_out_cotangent(jax.random.fold_in(splits[4], 71), 0),
    }


def head_gradients(head_args):
    query_rows, key_rows, value_rows, cotangent_rows = head_args
    score_scale = 1.0 / math.sqrt(DH)
    logits = jnp.dot(query_rows, key_rows.T, preferred_element_type=jnp.float32) * score_scale
    row_top = lax.optimization_barrier(jnp.max(logits, axis=1, keepdims=True))
    log_total = row_top + jnp.log(lax.optimization_barrier(jnp.sum(jnp.exp(logits - row_top), axis=1, keepdims=True)))
    weights = jnp.exp(logits - log_total)
    softmax_weights = weights.astype(jnp.bfloat16)
    weight_cotangent = jnp.dot(cotangent_rows, value_rows.T, preferred_element_type=jnp.float32)
    row_delta = lax.optimization_barrier(jnp.sum(softmax_weights.astype(jnp.float32) * weight_cotangent, axis=1, keepdims=True))
    score_cotangent = (weights * (weight_cotangent - row_delta)).astype(jnp.bfloat16)
    value_part = jnp.dot(softmax_weights.T, cotangent_rows, preferred_element_type=jnp.float32)
    key_part = jnp.dot(score_cotangent.T, query_rows, preferred_element_type=jnp.float32) * score_scale
    query_part = jnp.dot(score_cotangent, key_rows, preferred_element_type=jnp.float32) * score_scale
    return (query_part, key_part, value_part)

def reference(queries, keys, values, out_cotangent):
    query_heads = queries.reshape(HEADS, R, DH)
    query_total = jnp.zeros((HEADS, R, DH), jnp.float32)
    key_list = []
    value_list = []
    for doc_index in range(DOCS):
        key_heads = jnp.transpose(keys[doc_index].reshape(KEYS, HEADS, DH), (1, 0, 2))
        value_heads = jnp.transpose(values[doc_index].reshape(KEYS, HEADS, DH), (1, 0, 2))
        cotangent_heads = out_cotangent[doc_index].reshape(HEADS, R, DH)
        query_part, key_part, value_part = lax.map(head_gradients, (query_heads, key_heads, value_heads, cotangent_heads))
        query_total = query_total + query_part
        key_list.append(jnp.transpose(key_part, (1, 0, 2)).reshape(KEYS, HEADS * DH).astype(jnp.bfloat16))
        value_list.append(jnp.transpose(value_part, (1, 0, 2)).reshape(KEYS, HEADS * DH).astype(jnp.bfloat16))
    return (query_total.reshape(HEADS * R, DH), jnp.stack(key_list), jnp.stack(value_list))
```

```python
import math

import jax
import jax.numpy as jnp
from jax import lax
from jax.experimental import pallas as pl
from jax.experimental.pallas import tpu as pltpu
from jax.sharding import PartitionSpec as P

HEADS = 16
DH = 256
R = 768
DOCS = 4
MP = 64
Z = 8
K = MP // Z
PAIR = HEADS // K
BLOCK = 192
HALF = BLOCK // 2
POS = 64
HERE = K * POS
CHUNK = 256
CHUNKS = R // CHUNK
SCALE = 1.0 / math.sqrt(DH)
MESH = pl.DeviceIdType.MESH
F32 = jnp.float32
BF16 = jnp.bfloat16


def dot(a, b, dims):
    return lax.dot_general(a, b, (dims, ((), ())), preferred_element_type=F32)


def kernel(
    q_in, k_in, v_in, g_in,
    dq_out, dk_out, dv_out,
    kbuf, vbuf, qbuf, gbuf, pbuf, wbuf, p16, s16, dkst, dvst,
    dq32, dq16, crecv, zsend, zrecv, yrecv, mstat, lstat, dstat,
    own_sem, ksend, krecv, vsend, vrecv, qsend, qrecv, gsend, grecv,
    lsend, lrecv, dsend, drecv, dksend, dkrecv, dvsend, dvrecv,
    csend, crsem, zssem, zrsem, yssem, yrsem,
):
    dp, mp = lax.axis_index("dp"), lax.axis_index("mp")
    k, z = lax.div(mp, Z), lax.rem(mp, Z)
    core = lax.rem(dp, 2)
    sibling = dp + 1 - 2 * core
    right = k * Z + lax.rem(z + 1, Z)
    left = k * Z + lax.rem(z + Z - 1, Z)

    def remote(src, dst, ssem, rsem, where):
        return pltpu.make_async_remote_copy(
            src_ref=src, dst_ref=dst, send_sem=ssem, recv_sem=rsem, device_id=where, device_id_type=MESH
        )

    def mates(d):
        j = lax.rem(k + d, K)
        return j, (dp, j * Z + z)

    def ringmates(d):
        j = lax.rem(z + d, Z)
        return j, (dp, k * Z + j)

    def each(n, fn, first=1):
        def body(d, carry):
            fn(d)
            return carry

        lax.fori_loop(first, n, body, 0)

    barrier = pltpu.get_barrier_semaphore()

    def greet(where):
        pl.semaphore_signal(barrier, inc=1, device_id=where, device_id_type=MESH)

    each(K, lambda d: greet(mates(d)[1]))
    each(Z, lambda d: greet(ringmates(d)[1]))
    each(DOCS, lambda d: greet((lax.rem(dp + d, DOCS), mp)))
    pl.semaphore_wait(barrier, K - 1 + Z - 1 + DOCS - 1)

    streams = ((q_in, qbuf, qsend, qrecv), (g_in.at[0], gbuf, gsend, grecv))

    def rows_of(j, start=0, size=BLOCK):
        return pl.ds(pl.multiple_of(j * BLOCK + start, 32), size)

    def hop(stream, h, side):
        src_in, buf, ssem, rsem = stream
        j = lax.rem(z + (Z - h if side == 0 else h), Z)
        part = rows_of(j) if h < 3 else rows_of(j, side * HALF, HALF)
        src = src_in if h == 0 else buf.at[part]
        i = side * 4 + h
        return remote(src, buf.at[part], ssem.at[i], rsem.at[i], (dp, right if side == 0 else left))

    def key_copy(a, d):
        j, where = mates(d)
        src = k_in.at[0, :, pl.ds(pl.multiple_of((j * PAIR + a) * DH, DH), DH)]
        return remote(src, kbuf.at[a, pl.ds(pl.multiple_of(k * POS, POS), POS)], ksend.at[a, j], krecv.at[a, k], where)

    def value_copy(a, d):
        j, where = mates(d)
        src = v_in.at[0, :, pl.ds(pl.multiple_of((j * PAIR + a) * DH, DH), DH)]
        return remote(src, vbuf.at[a, pl.ds(pl.multiple_of(k * POS, POS), POS)], vsend.at[a, j], vrecv.at[a, k], where)

    for stream in streams:
        for side in range(2):
            hop(stream, 0, side).start()
    for a in range(PAIR):
        each(K, lambda d: key_copy(a, d).start())
        each(K, lambda d: value_copy(a, d).start())

    own = [
        pltpu.make_async_copy(q_in, qbuf.at[rows_of(z)], own_sem.at[0]),
        pltpu.make_async_copy(g_in.at[0], gbuf.at[rows_of(z)], own_sem.at[1]),
    ]
    for a in range(PAIR):
        cols = pl.ds(pl.multiple_of((k * PAIR + a) * DH, DH), DH)
        here = pl.ds(pl.multiple_of(k * POS, POS), POS)
        own.append(pltpu.make_async_copy(k_in.at[0, :, cols], kbuf.at[a, here], own_sem.at[2 + 2 * a]))
        own.append(pltpu.make_async_copy(v_in.at[0, :, cols], vbuf.at[a, here], own_sem.at[3 + 2 * a]))
    for copy in own:
        copy.start()

    for h in range(1, 4):
        for stream in streams:
            for side in range(2):
                hop(stream, h - 1, side).wait_recv()
                hop(stream, h, side).start()
    for copy in own:
        copy.wait()
    for stream in streams:
        for side in range(2):
            hop(stream, 3, side).wait_recv()
    for a in range(PAIR):
        def landed(d, a=a):
            j, where = mates(d)
            here = pl.ds(pl.multiple_of(j * POS, POS), POS)
            remote(kbuf.at[a, here], kbuf.at[a, here], ksend.at[a, j], krecv.at[a, j], where).wait_recv()
            remote(vbuf.at[a, here], vbuf.at[a, here], vsend.at[a, j], vrecv.at[a, j], where).wait_recv()

        each(K, landed)

    for a in range(PAIR):
        for c in range(CHUNKS):
            i = a * CHUNKS + c
            rows, cols = pl.ds(i * CHUNK, CHUNK), pl.ds(c * CHUNK, CHUNK)
            s = dot(kbuf[a], qbuf[rows, :], ((1,), (1,))) * SCALE
            top = jnp.max(s, axis=0, keepdims=True)
            p = jnp.exp(s - top)
            total = jnp.sum(p, axis=0, keepdims=True)
            w = dot(vbuf[a], gbuf[rows, :], ((1,), (1,)))
            delta = jnp.sum(p * w, axis=0, keepdims=True)
            pbuf[i] = p
            wbuf[i] = w
            mstat[a, :, cols] = top
            lstat[a, z, :, cols] = top + jnp.log(total)
            dstat[a, z, :, cols] = delta / total

        def stat_send(d, a=a):
            j, where = ringmates(d)
            remote(lstat.at[a, z], lstat.at[a, z], lsend.at[a, j], lrecv.at[a, z], where).start()
            remote(dstat.at[a, z], dstat.at[a, z], dsend.at[a, j], drecv.at[a, z], where).start()

        each(Z, stat_send)

    for a in range(PAIR):

        def stat_wait(d, a=a):
            j, where = ringmates(d)
            remote(lstat.at[a, j], lstat.at[a, j], lsend.at[a, j], lrecv.at[a, j], where).wait_recv()
            remote(dstat.at[a, j], dstat.at[a, j], dsend.at[a, j], drecv.at[a, j], where).wait_recv()

        each(Z, stat_wait)
        parts = [lstat[a, j] for j in range(Z)]
        peak = parts[0]
        for part in parts[1:]:
            peak = jnp.maximum(peak, part)
        shares = [jnp.exp(part - peak) for part in parts]
        whole = shares[0]
        for share in shares[1:]:
            whole = whole + share
        delta = shares[0] * dstat[a, 0]
        for j in range(1, Z):
            delta = delta + shares[j] * dstat[a, j]
        delta = delta / whole
        factor = jnp.exp(mstat[a] - (peak + jnp.log(whole)))
        for c in range(CHUNKS):
            i = a * CHUNKS + c
            rows = pl.ds(i * CHUNK, CHUNK)
            lo, hi = c * CHUNK, (c + 1) * CHUNK
            p = pbuf[i] * factor[:, lo:hi]
            s = (p * (wbuf[i] - delta[:, lo:hi])).astype(BF16)
            p16[a, :, lo:hi] = p.astype(BF16)
            s16[a, :, lo:hi] = s
            part = dot(s, kbuf[a], ((0,), (0,))) * SCALE
            dq32[rows, :] = part
            dq16[rows, :] = part.astype(BF16)

    def half_of(j, which):
        return pl.ds(pl.multiple_of(j * BLOCK + which * HALF, 32), HALF)

    def core_copy(j):
        return remote(dq16.at[half_of(j, 1 - core)], crecv.at[j], csend.at[j], crsem.at[j], (sibling, mp))

    each(Z, lambda j: core_copy(j).start(), 0)

    def key_back(a, d):
        j, where = mates(d)
        dst = dk_out.at[0, :, pl.ds(pl.multiple_of((k * PAIR + a) * DH, DH), DH)]
        src = dkst.at[a, pl.ds(pl.multiple_of(j * POS, POS), POS)]
        return remote(src, dst, dksend.at[a, j], dkrecv.at[a, k], where)

    def value_back(a, d):
        j, where = mates(d)
        dst = dv_out.at[0, :, pl.ds(pl.multiple_of((k * PAIR + a) * DH, DH), DH)]
        src = dvst.at[a, pl.ds(pl.multiple_of(j * POS, POS), POS)]
        return remote(src, dst, dvsend.at[a, j], dvrecv.at[a, k], where)

    kept = []
    for a in range(PAIR):
        rows = pl.ds(a * R, R)
        cols = pl.ds(pl.multiple_of((k * PAIR + a) * DH, DH), DH)
        here = pl.ds(pl.multiple_of(k * POS, POS), POS)
        dvst[a] = dot(p16[a], gbuf[rows, :], ((1,), (0,))).astype(BF16)
        each(K, lambda d, a=a: value_back(a, d).start())
        dkst[a] = (dot(s16[a], qbuf[rows, :], ((1,), (0,))) * SCALE).astype(BF16)
        each(K, lambda d, a=a: key_back(a, d).start())
        kept.append(pltpu.make_async_copy(dvst.at[a, here], dv_out.at[0, :, cols], own_sem.at[2 * a]))
        kept.append(pltpu.make_async_copy(dkst.at[a, here], dk_out.at[0, :, cols], own_sem.at[2 * a + 1]))
        for copy in kept[2 * a :]:
            copy.start()

    def z_copy(j):
        return remote(zsend.at[j], zrecv.at[z], zssem.at[j], zrsem.at[z], (dp, k * Z + j))

    def pass_on(d):
        j = lax.rem(z + d, Z)
        core_copy(j).wait_recv()
        zsend[j] = (dq32[half_of(j, core), :] + crecv[j].astype(F32)).astype(BF16)

        @pl.when(d < Z)
        def _():
            z_copy(j).start()

    each(Z + 1, pass_on)
    zrecv[z] = zsend[z]

    def z_wait(d):
        j = lax.rem(z + d, Z)
        remote(zsend.at[j], zrecv.at[j], zssem.at[j], zrsem.at[j], (dp, k * Z + j)).wait_recv()

    each(Z, z_wait)
    half_sum = zrecv[0].astype(F32)
    for j in range(1, Z):
        half_sum = half_sum + zrecv[j].astype(F32)
    yrecv[dp] = half_sum.astype(BF16)

    def y_copy(d):
        j = lax.rem(dp + d, DOCS)
        return remote(yrecv.at[dp], yrecv.at[dp], yssem.at[j], yrsem.at[dp], (j, mp))

    each(DOCS, lambda d: y_copy(d).start())

    def y_wait(d):
        j = lax.rem(dp + d, DOCS)
        remote(yrecv.at[j], yrecv.at[j], yssem.at[j], yrsem.at[j], (j, mp)).wait_recv()

    each(DOCS, y_wait)
    for h in range(2):
        dq_out[pl.ds(h * HALF, HALF), :] = yrecv[h].astype(F32) + yrecv[2 + h].astype(F32)

    for copy in kept:
        copy.wait()
    for stream in streams:
        for h in range(4):
            for side in range(2):
                hop(stream, h, side).wait_send()
    for a in range(PAIR):

        def settle(d, a=a):
            j, where = mates(d)
            cols = pl.ds(pl.multiple_of((j * PAIR + a) * DH, DH), DH)
            here = pl.ds(pl.multiple_of(j * POS, POS), POS)
            key_copy(a, d).wait_send()
            value_copy(a, d).wait_send()
            key_back(a, d).wait_send()
            value_back(a, d).wait_send()
            remote(dkst.at[a, here], dk_out.at[0, :, cols], dksend.at[a, j], dkrecv.at[a, j], where).wait_recv()
            remote(dvst.at[a, here], dv_out.at[0, :, cols], dvsend.at[a, j], dvrecv.at[a, j], where).wait_recv()

        each(K, settle)

        def settle_stats(d, a=a):
            j, where = ringmates(d)
            remote(lstat.at[a, z], lstat.at[a, z], lsend.at[a, j], lrecv.at[a, z], where).wait_send()
            remote(dstat.at[a, z], dstat.at[a, z], dsend.at[a, j], drecv.at[a, z], where).wait_send()

        each(Z, settle_stats)
    each(Z, lambda j: core_copy(j).wait_send(), 0)
    each(Z, lambda d: z_copy(lax.rem(z + d, Z)).wait_send())
    each(DOCS, lambda d: y_copy(d).wait_send())


def on_device(queries, keys, values, out_cotangent):
    anywhere = pl.BlockSpec(memory_space=pl.ANY)
    dma = pltpu.SemaphoreType.DMA
    return pl.pallas_call(
        kernel,
        out_shape=(
            jax.ShapeDtypeStruct((BLOCK, DH), F32),
            jax.ShapeDtypeStruct(keys.shape, BF16),
            jax.ShapeDtypeStruct(values.shape, BF16),
        ),
        in_specs=[anywhere] * 4,
        out_specs=(pl.BlockSpec(memory_space=pltpu.VMEM), anywhere, anywhere),
        scratch_shapes=[
            pltpu.VMEM((PAIR, HERE, DH), BF16),
            pltpu.VMEM((PAIR, HERE, DH), BF16),
            pltpu.VMEM((PAIR * R, DH), BF16),
            pltpu.VMEM((PAIR * R, DH), BF16),
            pltpu.VMEM((PAIR * CHUNKS, HERE, CHUNK), F32),
            pltpu.VMEM((PAIR * CHUNKS, HERE, CHUNK), F32),
            pltpu.VMEM((PAIR, HERE, R), BF16),
            pltpu.VMEM((PAIR, HERE, R), BF16),
            pltpu.VMEM((PAIR, HERE, DH), BF16),
            pltpu.VMEM((PAIR, HERE, DH), BF16),
            pltpu.VMEM((PAIR * R, DH), F32),
            pltpu.VMEM((PAIR * R, DH), BF16),
            pltpu.VMEM((Z, HALF, DH), BF16),
            pltpu.VMEM((Z, HALF, DH), BF16),
            pltpu.VMEM((Z, HALF, DH), BF16),
            pltpu.VMEM((DOCS, HALF, DH), BF16),
            pltpu.VMEM((PAIR, 1, R), F32),
            pltpu.VMEM((PAIR, Z, 1, R), F32),
            pltpu.VMEM((PAIR, Z, 1, R), F32),
            dma((6,)),
            dma((PAIR, K)), dma((PAIR, K)), dma((PAIR, K)), dma((PAIR, K)),
            dma((8,)), dma((8,)), dma((8,)), dma((8,)),
            dma((PAIR, Z)), dma((PAIR, Z)), dma((PAIR, Z)), dma((PAIR, Z)),
            dma((PAIR, K)), dma((PAIR, K)), dma((PAIR, K)), dma((PAIR, K)),
            dma((Z,)), dma((Z,)), dma((Z,)), dma((Z,)), dma((DOCS,)), dma((DOCS,)),
        ],
        compiler_params=pltpu.CompilerParams(
            collective_id=0, has_side_effects=True, vmem_limit_bytes=48 * 2**20
        ),
        cost_estimate=pl.CostEstimate(
            flops=10 * HERE * PAIR * R * DH, bytes_accessed=4 * 2**20, transcendentals=HERE * PAIR * R
        ),
    )(queries, keys, values, out_cotangent)


def solution(mesh):
    placed = (P("mp", None), P("dp", "mp", None), P("dp", "mp", None), P("dp", "mp", None))
    return jax.shard_map(
        on_device,
        mesh=mesh,
        in_specs=placed,
        out_specs=(P("mp", None), P("dp", "mp", None), P("dp", "mp", None)),
        check_vma=False,
    )
```

```python
import math

import jax
import jax.numpy as jnp
from jax import lax
from jax.experimental import pallas as pl
from jax.experimental.pallas import tpu as pltpu
from jax.sharding import PartitionSpec as P

HEADS = 16
DH = 256
R = 768
DOCS = 4
MP = 64
Z = 8
K = MP // Z
PAIR = HEADS // K
BLOCK = 192
HALF = BLOCK // 2
POS = 64
HERE = K * POS
CHUNK = 256
CHUNKS = R // CHUNK
SCALE = 1.0 / math.sqrt(DH)
MESH = pl.DeviceIdType.MESH
F32 = jnp.float32
BF16 = jnp.bfloat16


def dot(a, b, dims):
    return lax.dot_general(a, b, (dims, ((), ())), preferred_element_type=F32)


def kernel(
    q_in, k_in, v_in, g_in,
    yrecv, dk_out, dv_out,
    kbuf, vbuf, qbuf, gbuf, pbuf, wbuf, p16, s16, dkst, dvst,
    dq32, dq16, crecv, zsend, zrecv, mstat, stat,
    own_sem, ksem, vsem, rsend, rrecv, shsem, stsem, dksem, dvsem, csend, crsem, zsem, ysem,
):
    dp, mp = lax.axis_index("dp"), lax.axis_index("mp")
    k, z = lax.div(mp, Z), lax.rem(mp, Z)
    core = lax.rem(dp, 2)
    sibling = dp + 1 - 2 * core
    right = k * Z + lax.rem(z + 1, Z)
    left = k * Z + lax.rem(z + Z - 1, Z)

    def remote(src, dst, ssem, rsem, where):
        return pltpu.make_async_remote_copy(
            src_ref=src, dst_ref=dst, send_sem=ssem, recv_sem=rsem, device_id=where, device_id_type=MESH
        )

    def mate(d):
        j = lax.rem(k + d, K)
        return j, (dp, j * Z + z)

    def ringmate(d):
        j = lax.rem(z + d, Z)
        return j, (dp, k * Z + j)

    def doc(d):
        j = lax.rem(dp + d, DOCS)
        return j, (j, mp)

    barrier = pltpu.get_barrier_semaphore()
    for others, count in ((mate, K), (ringmate, Z), (doc, DOCS)):
        for d in range(1, count):
            pl.semaphore_signal(barrier, inc=1, device_id=others(d)[1], device_id_type=MESH)
    pl.semaphore_wait(barrier, K - 1 + Z - 1 + DOCS - 1)

    def rows_of(j, start, size):
        return pl.ds(pl.multiple_of(j * BLOCK + start, 16), size)

    def cols_of(j):
        return pl.ds(pl.multiple_of(j * PAIR * DH, PAIR * DH), PAIR * DH)

    def pos_of(j):
        return pl.ds(pl.multiple_of(j * POS, POS), POS)

    def hop(part, h, side):
        buf, first = (qbuf, q_in) if part == 0 else (gbuf, g_in.at[0])
        start, size = (core * HALF, HALF) if part == 0 else ((part - 1) * HALF, HALF)
        if h == 3 and part == 0:
            start, size = start + side * (HALF // 2), HALF // 2
        j = lax.rem(z + (Z - h if side == 0 else h), Z)
        there = buf.at[rows_of(j, start, size)]
        src = first.at[pl.ds(pl.multiple_of(start, 16), size)] if h == 0 else there
        i = (part * 2 + side) * 4 + h
        return remote(src, there, rsend.at[i], rrecv.at[i], (dp, right if side == 0 else left))

    def travels(part, h, side):
        return h < 3 or part == 0 or part == side + 1

    def share(h, side):
        j = lax.rem(z + (Z - 1 - h if side == 0 else h + 1), Z)
        start, size = (core * HALF, HALF) if h < 3 else (core * HALF + side * (HALF // 2), HALF // 2)
        there = qbuf.at[rows_of(j, start, size)]
        return remote(there, there, shsem.at[0], shsem.at[1], (sibling, mp))

    def shared():
        there = qbuf.at[pl.ds(0, (Z - 1) * HALF)]
        return remote(there, there, shsem.at[0], shsem.at[1], (sibling, mp))

    for part in range(3):
        for side in range(2):
            hop(part, 0, side).start()

    for src, buf, sem in ((k_in, kbuf, ksem), (v_in, vbuf, vsem)):
        for d in range(1, K):
            j, where = mate(d)
            remote(src.at[0, :, cols_of(j)], buf.at[pos_of(k)], sem.at[0], sem.at[1], where).start()

    own = [
        pltpu.make_async_copy(q_in, qbuf.at[rows_of(z, 0, BLOCK)], own_sem.at[0]),
        pltpu.make_async_copy(g_in.at[0], gbuf.at[rows_of(z, 0, BLOCK)], own_sem.at[1]),
        pltpu.make_async_copy(k_in.at[0, :, cols_of(k)], kbuf.at[pos_of(k)], own_sem.at[2]),
        pltpu.make_async_copy(v_in.at[0, :, cols_of(k)], vbuf.at[pos_of(k)], own_sem.at[3]),
    ]
    for copy in own:
        copy.start()

    for h in range(1, 5):
        for part in range(3):
            for side in range(2):
                if travels(part, h - 1, side):
                    hop(part, h - 1, side).wait_recv()
                    if h < 4 and travels(part, h, side):
                        hop(part, h, side).start()
                    if part == 0:
                        share(h - 1, side).start()

    def all_mates(buf, sem):
        there = buf.at[pl.ds(0, (K - 1) * POS)]
        return remote(there, there, sem.at[0], sem.at[1], mate(1)[1])

    for copy in own:
        copy.wait()
    shared().wait_recv()
    all_mates(kbuf, ksem).wait_recv()
    all_mates(vbuf, vsem).wait_recv()

    for a in range(PAIR):
        head = pl.ds(a * DH, DH)
        for c in range(CHUNKS):
            i = a * CHUNKS + c
            rows, cols = pl.ds(i * CHUNK, CHUNK), pl.ds(c * CHUNK, CHUNK)
            s = dot(kbuf[:, head], qbuf[rows, :], ((1,), (1,))) * SCALE
            top = jnp.max(s, axis=0, keepdims=True)
            p = jnp.exp(s - top)
            total = jnp.sum(p, axis=0, keepdims=True)
            w = dot(vbuf[:, head], gbuf[rows, :], ((1,), (1,)))
            delta = jnp.sum(p * w, axis=0, keepdims=True)
            pbuf[i] = p
            wbuf[i] = w
            mstat[a, :, cols] = top
            stat[z, 2 * a, :, cols] = top + jnp.log(total)
            stat[z, 2 * a + 1, :, cols] = delta / total

    for d in (4, 3, 5, 2, 6, 1, 7):
        j, where = ringmate(d)
        remote(stat.at[z], stat.at[z], stsem.at[0], stsem.at[1], where).start()

    def all_stats():
        there = stat.at[pl.ds(0, Z - 1)]
        return remote(there, there, stsem.at[0], stsem.at[1], ringmate(1)[1])

    all_stats().wait_recv()

    def core_copy(a):
        mine = pl.ds(pl.multiple_of((1 - core) * HALF, HALF), HALF)
        there = pl.ds(a * (Z // 2), Z // 2)
        return remote(dq16.at[there, mine], crecv.at[there], csend.at[a], crsem.at[a], (sibling, mp))

    for a in range(PAIR):
        head = pl.ds(a * DH, DH)
        parts = [stat[j, 2 * a] for j in range(Z)]
        peak = parts[0]
        for part in parts[1:]:
            peak = jnp.maximum(peak, part)
        shares = [jnp.exp(part - peak) for part in parts]
        whole = shares[0]
        for part in shares[1:]:
            whole = whole + part
        delta = shares[0] * stat[0, 2 * a + 1]
        for j in range(1, Z):
            delta = delta + shares[j] * stat[j, 2 * a + 1]
        delta = delta / whole
        factor = jnp.exp(mstat[a] - (peak + jnp.log(whole)))
        for c in range(CHUNKS):
            i = a * CHUNKS + c
            lo, hi = c * CHUNK, (c + 1) * CHUNK
            p = pbuf[i] * factor[:, lo:hi]
            p16[a, :, lo:hi] = p.astype(BF16)
            s16[a, :, lo:hi] = (p * (wbuf[i] - delta[:, lo:hi])).astype(BF16)
        there = pl.ds(a * (Z // 2), Z // 2)
        part = (dot(s16[a], kbuf[:, head], ((0,), (0,))) * SCALE).reshape(Z // 2, BLOCK, DH)
        dq32[there] = part
        dq16[there] = part.astype(BF16)
        core_copy(a).start()

    def back(stage, out, sem, values_of):
        for a in range(PAIR):
            stage[:, a * DH : (a + 1) * DH] = values_of(a).astype(BF16)
        for d in range(1, K):
            j, where = mate(d)
            remote(stage.at[pos_of(j)], out.at[0, :, cols_of(k)], sem.at[0], sem.at[1], where).start()

    back(dvst, dv_out, dvsem, lambda a: dot(p16[a], gbuf[pl.ds(a * R, R), :], ((1,), (0,))))

    def z_copy(j):
        return remote(zsend.at[j], zrecv.at[z], zsem.at[0], zsem.at[1], (dp, k * Z + j))

    for a in range(PAIR):
        core_copy(a).wait_recv()
    for d in (4, 3, 5, 2, 6, 1, 7, 0):
        j = lax.rem(z + d, Z)
        mine = pl.ds(pl.multiple_of(core * HALF, HALF), HALF)
        part = (dq32[j, mine, :] + crecv[j].astype(F32)).astype(BF16)
        if d:
            zsend[j] = part
            z_copy(j).start()
        else:
            zrecv[j] = part

    back(dkst, dk_out, dksem, lambda a: dot(s16[a], qbuf[pl.ds(a * R, R), :], ((1,), (0,))) * SCALE)
    kept = [
        pltpu.make_async_copy(dvst.at[pos_of(k)], dv_out.at[0, :, cols_of(k)], own_sem.at[0]),
        pltpu.make_async_copy(dkst.at[pos_of(k)], dk_out.at[0, :, cols_of(k)], own_sem.at[1]),
    ]
    for copy in kept:
        copy.start()

    for part in range(3):
        for h in range(4):
            for side in range(2):
                if travels(part, h, side):
                    hop(part, h, side).wait_send()
    shared().wait_send()
    all_mates(kbuf, ksem).wait_send()
    all_mates(vbuf, vsem).wait_send()
    all_stats().wait_send()
    for a in range(PAIR):
        core_copy(a).wait_send()

    def all_z():
        there = zrecv.at[pl.ds(0, Z - 1)]
        return remote(there, there, zsem.at[0], zsem.at[1], ringmate(1)[1])

    all_z().wait_recv()
    half_sum = zrecv[0].astype(F32)
    for j in range(1, Z):
        half_sum = half_sum + zrecv[j].astype(F32)
    yrecv[dp] = half_sum.astype(BF16)

    for d in range(1, DOCS):
        remote(yrecv.at[dp], yrecv.at[dp], ysem.at[0], ysem.at[1], doc(d)[1]).start()

    def all_docs():
        there = yrecv.at[pl.ds(0, DOCS - 1)]
        return remote(there, there, ysem.at[0], ysem.at[1], doc(1)[1])

    all_docs().wait_recv()
    for copy in kept:
        copy.wait()
    for out, sem in ((dv_out, dvsem), (dk_out, dksem)):
        there = out.at[0, :, pl.ds(0, (K - 1) * PAIR * DH)]
        done = remote(there, there, sem.at[0], sem.at[1], mate(1)[1])
        done.wait_send()
        done.wait_recv()
    all_z().wait_send()
    all_docs().wait_send()


def finish(parts, dk_in, dv_in, dq_out, dk_out, dv_out, sem):
    copies = [
        pltpu.make_async_copy(dk_in, dk_out, sem.at[0]),
        pltpu.make_async_copy(dv_in, dv_out, sem.at[1]),
    ]
    for copy in copies:
        copy.start()
    for h in range(2):
        dq_out[pl.ds(h * HALF, HALF), :] = parts[h].astype(F32) + parts[2 + h].astype(F32)
    for copy in copies:
        copy.wait()


def on_device(queries, keys, values, out_cotangent):
    queries, keys, values, out_cotangent = (
        pltpu.with_memory_space_constraint(x, pltpu.HBM) for x in (queries, keys, values, out_cotangent)
    )
    anywhere = pl.BlockSpec(memory_space=pl.ANY)
    dma = pltpu.SemaphoreType.DMA
    parts, key_gradient, value_gradient = pl.pallas_call(
        kernel,
        out_shape=(
            pltpu.VMEM((DOCS, HALF, DH), BF16),
            pltpu.VMEM(keys.shape, BF16),
            pltpu.VMEM(values.shape, BF16),
        ),
        in_specs=[anywhere] * 4,
        out_specs=[pl.BlockSpec(memory_space=pltpu.VMEM)] * 3,
        scratch_shapes=[
            pltpu.VMEM((HERE, PAIR * DH), BF16),
            pltpu.VMEM((HERE, PAIR * DH), BF16),
            pltpu.VMEM((PAIR * R, DH), BF16),
            pltpu.VMEM((PAIR * R, DH), BF16),
            pltpu.VMEM((PAIR * CHUNKS, HERE, CHUNK), F32),
            pltpu.VMEM((PAIR * CHUNKS, HERE, CHUNK), F32),
            pltpu.VMEM((PAIR, HERE, R), BF16),
            pltpu.VMEM((PAIR, HERE, R), BF16),
            pltpu.VMEM((HERE, PAIR * DH), BF16),
            pltpu.VMEM((HERE, PAIR * DH), BF16),
            pltpu.VMEM((Z, BLOCK, DH), F32),
            pltpu.VMEM((Z, BLOCK, DH), BF16),
            pltpu.VMEM((Z, HALF, DH), BF16),
            pltpu.VMEM((Z, HALF, DH), BF16),
            pltpu.VMEM((Z, HALF, DH), BF16),
            pltpu.VMEM((PAIR, 1, R), F32),
            pltpu.VMEM((Z, 2 * PAIR, 1, R), F32),
            dma((4,)), dma((2,)), dma((2,)), dma((24,)), dma((24,)), dma((2,)), dma((2,)),
            dma((2,)), dma((2,)), dma((PAIR,)), dma((PAIR,)), dma((2,)), dma((2,)),
        ],
        compiler_params=pltpu.CompilerParams(
            collective_id=0, has_side_effects=True, vmem_limit_bytes=48 * 2**20
        ),
        cost_estimate=pl.CostEstimate(
            flops=10 * HERE * PAIR * R * DH, bytes_accessed=4 * 2**20, transcendentals=HERE * PAIR * R
        ),
    )(queries, keys, values, out_cotangent)
    return pl.pallas_call(
        finish,
        out_shape=(
            jax.ShapeDtypeStruct((BLOCK, DH), F32),
            jax.ShapeDtypeStruct(keys.shape, BF16),
            jax.ShapeDtypeStruct(values.shape, BF16),
        ),
        in_specs=[pl.BlockSpec(memory_space=pltpu.VMEM)] * 3,
        out_specs=(pl.BlockSpec(memory_space=pltpu.VMEM), anywhere, anywhere),
        scratch_shapes=[dma((2,))],
        compiler_params=pltpu.CompilerParams(vmem_limit_bytes=4 * 2**20),
    )(parts, key_gradient, value_gradient)


def solution(mesh):
    placed = (P("mp", None), P("dp", "mp", None), P("dp", "mp", None), P("dp", "mp", None))
    return jax.shard_map(
        on_device,
        mesh=mesh,
        in_specs=placed,
        out_specs=(P("mp", None), P("dp", "mp", None), P("dp", "mp", None)),
        check_vma=False,
    )
```

```python
import math

import jax
import jax.numpy as jnp
from jax import lax
from jax.experimental import pallas as pl
from jax.experimental.pallas import tpu as pltpu
from jax.sharding import PartitionSpec as P

HEADS = 16
DH = 256
R = 768
DOCS = 4
MP = 64
Z = 8
K = MP // Z
PAIR = HEADS // K
BLOCK = 192
HALF = BLOCK // 2
POS = 64
HERE = K * POS
WIDE = 2 * BLOCK
WIDES = PAIR * R // WIDE
SCALE = 1.0 / math.sqrt(DH)
MESH = pl.DeviceIdType.MESH
F32 = jnp.float32
BF16 = jnp.bfloat16


def dot(a, b, dims):
    return lax.dot_general(a, b, (dims, ((), ())), preferred_element_type=F32)


def kernel(
    q_in, k_in, v_in, g_in,
    yrecv, dk_out, dv_out,
    kbuf, vbuf, qbuf, gbuf, pbuf, wbuf, p16, s16, aq, bq, dkst, dvst,
    dq32, dq16, crecv, zsend, zrecv, mstat, tstat, logs, deltas,
    own_sem, ksem, vsem, rsend, rrecv, shsem, lsem, dsem, dksem, dvsem, csend, crsem, zsem, ysem,
):
    dp, mp = lax.axis_index("dp"), lax.axis_index("mp")
    k, z = lax.div(mp, Z), lax.rem(mp, Z)
    core = lax.rem(dp, 2)
    sibling = dp + 1 - 2 * core
    right = k * Z + lax.rem(z + 1, Z)
    left = k * Z + lax.rem(z + Z - 1, Z)

    def remote(src, dst, ssem, rsem, where):
        return pltpu.make_async_remote_copy(
            src_ref=src, dst_ref=dst, send_sem=ssem, recv_sem=rsem, device_id=where, device_id_type=MESH
        )

    def mate(d):
        j = lax.rem(k + d, K)
        return j, (dp, j * Z + z)

    def ringmate(d):
        j = lax.rem(z + d, Z)
        return j, (dp, k * Z + j)

    def doc(d):
        j = lax.rem(dp + d, DOCS)
        return j, (j, mp)

    barrier = pltpu.get_barrier_semaphore()
    partners = [mate(d)[1] for d in range(1, K)] + [doc(d)[1] for d in range(1, DOCS)] + [(dp, right), (dp, left)]
    for where in partners:
        pl.semaphore_signal(barrier, inc=1, device_id=where, device_id_type=MESH)
    pl.semaphore_wait(barrier, len(partners))

    def rows_of(j, start, size):
        return pl.ds(pl.multiple_of(j * BLOCK + start, 16), size)

    def cols_of(j):
        return pl.ds(pl.multiple_of(j * PAIR * DH, PAIR * DH), PAIR * DH)

    def pos_of(j):
        return pl.ds(pl.multiple_of(j * POS, POS), POS)

    def hop(part, h, side):
        buf, first = (qbuf, q_in) if part == 0 else (gbuf, g_in.at[0])
        start, size = (core * HALF, HALF) if part == 0 else ((part - 1) * HALF, HALF)
        if h == 3 and part == 0:
            start, size = start + side * (HALF // 2), HALF // 2
        j = lax.rem(z + (Z - h if side == 0 else h), Z)
        there = buf.at[rows_of(j, start, size)]
        src = first.at[pl.ds(pl.multiple_of(start, 16), size)] if h == 0 else there
        i = (part * 2 + side) * 4 + h
        return remote(src, there, rsend.at[i], rrecv.at[i], (dp, right if side == 0 else left))

    def travels(part, h, side):
        return h < 3 or part == 0 or part == side + 1

    def share(h, side):
        j = lax.rem(z + (Z - 1 - h if side == 0 else h + 1), Z)
        start, size = (core * HALF, HALF) if h < 3 else (core * HALF + side * (HALF // 2), HALF // 2)
        there = qbuf.at[rows_of(j, start, size)]
        return remote(there, there, shsem.at[0], shsem.at[1 + h // 3], (sibling, mp))

    def shared(last):
        there = qbuf.at[pl.ds(0, HALF if last else 6 * HALF)]
        return remote(there, there, shsem.at[0], shsem.at[1 + last], (sibling, mp))

    for part in range(3):
        for side in range(2):
            hop(part, 0, side).start()

    for src, buf, sem in ((k_in, kbuf, ksem), (v_in, vbuf, vsem)):
        for d in range(1, K):
            j, where = mate(d)
            remote(src.at[0, :, cols_of(j)], buf.at[pos_of(k)], sem.at[0], sem.at[1], where).start()

    own = [
        pltpu.make_async_copy(q_in, qbuf.at[rows_of(z, 0, BLOCK)], own_sem.at[0]),
        pltpu.make_async_copy(g_in.at[0], gbuf.at[rows_of(z, 0, BLOCK)], own_sem.at[1]),
        pltpu.make_async_copy(k_in.at[0, :, cols_of(k)], kbuf.at[pos_of(k)], own_sem.at[2]),
        pltpu.make_async_copy(v_in.at[0, :, cols_of(k)], vbuf.at[pos_of(k)], own_sem.at[3]),
    ]
    for copy in own:
        copy.start()

    for h in range(1, 4):
        for part in range(3):
            for side in range(2):
                hop(part, h - 1, side).wait_recv()
                if travels(part, h, side):
                    hop(part, h, side).start()
                if part == 0:
                    share(h - 1, side).start()

    def all_mates(buf, sem):
        there = buf.at[pl.ds(0, (K - 1) * POS)]
        return remote(there, there, sem.at[0], sem.at[1], mate(1)[1])

    def place(w):
        a = lax.div(w, 2)
        head = pl.ds(pl.multiple_of(a * DH, DH), DH)
        rows = pl.ds(pl.multiple_of(w * WIDE, WIDE), WIDE)
        cols = pl.ds(pl.multiple_of(lax.rem(w, 2) * WIDE, WIDE), WIDE)
        return a, head, rows, cols

    def score(w):
        a, head, rows, cols = place(w)
        s = dot(kbuf[:, head], qbuf[rows, :], ((1,), (1,))) * SCALE
        top = jnp.max(s, axis=0, keepdims=True)
        p = jnp.exp(s - top)
        total = jnp.sum(p, axis=0, keepdims=True)
        pbuf[w] = p
        p16[a, :, cols] = p.astype(BF16)
        mstat[a, :, cols] = top
        tstat[a, :, cols] = total
        logs[z, a, :, cols] = top + jnp.log(total)

    def weigh(w):
        a, head, rows, cols = place(w)
        c = dot(vbuf[:, head], gbuf[rows, :], ((1,), (1,)))
        wbuf[w] = c
        deltas[z, a, :, cols] = jnp.sum(pbuf[w] * c, axis=0, keepdims=True) / tstat[a, :, cols]

    def settle(w):
        a, head, rows, cols = place(w)
        s16[a, :, cols] = (pbuf[w] * (wbuf[w] - deltas[z, a, :, cols])).astype(BF16)

    pair = lax.div(z, 2)
    early = [pair, lax.rem(pair + 1, WIDES), lax.rem(pair + 3, WIDES)]
    late = lax.rem(pair + 2, WIDES)
    for copy in own:
        copy.wait()
    shared(0).wait_recv()
    all_mates(kbuf, ksem).wait_recv()
    for w in early:
        score(w)
    for side in range(2):
        hop(0, 3, side).wait_recv()
        share(3, side).start()
    all_mates(vbuf, vsem).wait_recv()
    for w in early:
        weigh(w)
        settle(w)
    def tell(stat, sem):
        for d in (4, 3, 5, 2, 6, 1, 7):
            remote(stat.at[z], stat.at[z], sem.at[0], sem.at[1], ringmate(d)[1]).start()

    def told(stat, sem):
        there = stat.at[pl.ds(0, Z - 1)]
        return remote(there, there, sem.at[0], sem.at[1], ringmate(1)[1])

    shared(1).wait_recv()
    score(late)
    tell(logs, lsem)
    for side in range(2):
        hop(side + 1, 3, side).wait_recv()
    weigh(late)
    tell(deltas, dsem)
    settle(late)
    for a in range(PAIR):
        there = kbuf[:, a * DH : (a + 1) * DH]
        aq[a] = dot(s16[a], there, ((0,), (0,)))
        bq[a] = dot(p16[a], there, ((0,), (0,)))

    def columns(rows):
        return jnp.concatenate(rows + [jnp.zeros((8 - len(rows), R), F32)], axis=0).T

    def back(stage, out, sem, values_of):
        for a in range(PAIR):
            stage[:, a * DH : (a + 1) * DH] = values_of(a).astype(BF16)
        for d in range(1, K):
            j, where = mate(d)
            remote(stage.at[pos_of(j)], out.at[0, :, cols_of(k)], sem.at[0], sem.at[1], where).start()

    told(logs, lsem).wait_recv()
    weights, factors = [], []
    for a in range(PAIR):
        parts = [logs[j, a] for j in range(Z)]
        peak = parts[0]
        for part in parts[1:]:
            peak = jnp.maximum(peak, part)
        shares = [jnp.exp(part - peak) for part in parts]
        whole = shares[0]
        for part in shares[1:]:
            whole = whole + part
        weights.append([share / whole for share in shares])
        factors.append(jnp.exp(mstat[a] - (peak + jnp.log(whole))))
    factor = columns(factors)

    def value_part(a):
        rows = gbuf[pl.ds(a * R, R), :].astype(F32) * factor[:, a : a + 1]
        return dot(p16[a], rows.astype(BF16), ((1,), (0,)))

    back(dvst, dv_out, dvsem, value_part)

    def core_copy(a):
        mine = pl.ds(pl.multiple_of((1 - core) * HALF, HALF), HALF)
        there = pl.ds(a * (Z // 2), Z // 2)
        return remote(dq16.at[there, mine], crecv.at[there], csend.at[a], crsem.at[a], (sibling, mp))

    told(deltas, dsem).wait_recv()
    changes = []
    for a in range(PAIR):
        delta = weights[a][0] * deltas[0, a]
        for j in range(1, Z):
            delta = delta + weights[a][j] * deltas[j, a]
        changes.append(factors[a] * (deltas[z, a] - delta))
    change = columns(changes)

    def query_part(a):
        there = pl.ds(a * (Z // 2), Z // 2)
        part = (factor[:, a : a + 1] * aq[a] + change[:, a : a + 1] * bq[a]) * SCALE
        part = part.reshape(Z // 2, BLOCK, DH)
        dq32[there] = part
        dq16[there] = part.astype(BF16)
        core_copy(a).start()

    def key_part(a):
        rows = qbuf[pl.ds(a * R, R), :].astype(F32)
        main = (rows * (factor[:, a : a + 1] * SCALE)).astype(BF16)
        rest = (rows * (change[:, a : a + 1] * SCALE)).astype(BF16)
        return dot(s16[a], main, ((1,), (0,))) + dot(p16[a], rest, ((1,), (0,)))

    def z_copy(j):
        return remote(zsend.at[j], zrecv.at[z], zsem.at[0], zsem.at[1], (dp, k * Z + j))

    def over_z(a):
        core_copy(a).wait_recv()
        mine = pl.ds(pl.multiple_of(core * HALF, HALF), HALF)
        for c in range(Z // 2):
            j = a * (Z // 2) + lax.rem(z + 2 + c, Z // 2)
            zsend[j] = (dq32[j, mine, :] + crecv[j].astype(F32)).astype(BF16)

            @pl.when(j != z)
            def _():
                z_copy(j).start()

            @pl.when(j == z)
            def _():
                zrecv[z] = zsend[z]

    query_part(0)
    query_part(1)
    over_z(0)
    over_z(1)
    back(dkst, dk_out, dksem, key_part)
    kept = [
        pltpu.make_async_copy(dvst.at[pos_of(k)], dv_out.at[0, :, cols_of(k)], own_sem.at[0]),
        pltpu.make_async_copy(dkst.at[pos_of(k)], dk_out.at[0, :, cols_of(k)], own_sem.at[1]),
    ]
    for copy in kept:
        copy.start()

    for part in range(3):
        for h in range(4):
            for side in range(2):
                if travels(part, h, side):
                    hop(part, h, side).wait_send()
    shared(0).wait_send()
    shared(1).wait_send()
    all_mates(kbuf, ksem).wait_send()
    all_mates(vbuf, vsem).wait_send()
    told(logs, lsem).wait_send()
    told(deltas, dsem).wait_send()
    for a in range(PAIR):
        core_copy(a).wait_send()

    def all_z():
        there = zrecv.at[pl.ds(0, Z - 1)]
        return remote(there, there, zsem.at[0], zsem.at[1], ringmate(1)[1])

    all_z().wait_recv()
    half_sum = zrecv[0].astype(F32)
    for j in range(1, Z):
        half_sum = half_sum + zrecv[j].astype(F32)
    yrecv[dp] = half_sum.astype(BF16)

    for d in range(1, DOCS):
        remote(yrecv.at[dp], yrecv.at[dp], ysem.at[0], ysem.at[1], doc(d)[1]).start()

    def all_docs():
        there = yrecv.at[pl.ds(0, DOCS - 1)]
        return remote(there, there, ysem.at[0], ysem.at[1], doc(1)[1])

    all_docs().wait_recv()
    for copy in kept:
        copy.wait()
    for out, sem in ((dv_out, dvsem), (dk_out, dksem)):
        there = out.at[0, :, pl.ds(0, (K - 1) * PAIR * DH)]
        done = remote(there, there, sem.at[0], sem.at[1], mate(1)[1])
        done.wait_send()
        done.wait_recv()
    all_z().wait_send()
    all_docs().wait_send()


def finish(parts, dk_in, dv_in, dq_out, dk_out, dv_out, sem):
    copies = [
        pltpu.make_async_copy(dk_in, dk_out, sem.at[0]),
        pltpu.make_async_copy(dv_in, dv_out, sem.at[1]),
    ]
    for copy in copies:
        copy.start()
    for h in range(2):
        dq_out[pl.ds(h * HALF, HALF), :] = parts[h].astype(F32) + parts[2 + h].astype(F32)
    for copy in copies:
        copy.wait()


def on_device(queries, keys, values, out_cotangent):
    queries, keys, values, out_cotangent = (
        pltpu.with_memory_space_constraint(x, pltpu.HBM) for x in (queries, keys, values, out_cotangent)
    )
    anywhere = pl.BlockSpec(memory_space=pl.ANY)
    dma = pltpu.SemaphoreType.DMA
    parts, key_gradient, value_gradient = pl.pallas_call(
        kernel,
        out_shape=(
            pltpu.VMEM((DOCS, HALF, DH), BF16),
            pltpu.VMEM(keys.shape, BF16),
            pltpu.VMEM(values.shape, BF16),
        ),
        in_specs=[anywhere] * 4,
        out_specs=[pl.BlockSpec(memory_space=pltpu.VMEM)] * 3,
        scratch_shapes=[
            pltpu.VMEM((HERE, PAIR * DH), BF16),
            pltpu.VMEM((HERE, PAIR * DH), BF16),
            pltpu.VMEM((PAIR * R, DH), BF16),
            pltpu.VMEM((PAIR * R, DH), BF16),
            pltpu.VMEM((WIDES, HERE, WIDE), F32),
            pltpu.VMEM((WIDES, HERE, WIDE), F32),
            pltpu.VMEM((PAIR, HERE, R), BF16),
            pltpu.VMEM((PAIR, HERE, R), BF16),
            pltpu.VMEM((PAIR, R, DH), F32),
            pltpu.VMEM((PAIR, R, DH), F32),
            pltpu.VMEM((HERE, PAIR * DH), BF16),
            pltpu.VMEM((HERE, PAIR * DH), BF16),
            pltpu.VMEM((Z, BLOCK, DH), F32),
            pltpu.VMEM((Z, BLOCK, DH), BF16),
            pltpu.VMEM((Z, HALF, DH), BF16),
            pltpu.VMEM((Z, HALF, DH), BF16),
            pltpu.VMEM((Z, HALF, DH), BF16),
            pltpu.VMEM((PAIR, 1, R), F32),
            pltpu.VMEM((PAIR, 1, R), F32),
            pltpu.VMEM((Z, PAIR, 1, R), F32),
            pltpu.VMEM((Z, PAIR, 1, R), F32),
            dma((4,)), dma((2,)), dma((2,)), dma((24,)), dma((24,)), dma((3,)), dma((2,)), dma((2,)),
            dma((2,)), dma((2,)), dma((PAIR,)), dma((PAIR,)), dma((2,)), dma((2,)),
        ],
        compiler_params=pltpu.CompilerParams(
            collective_id=0, has_side_effects=True, vmem_limit_bytes=48 * 2**20
        ),
        cost_estimate=pl.CostEstimate(
            flops=10 * HERE * PAIR * R * DH, bytes_accessed=4 * 2**20, transcendentals=HERE * PAIR * R
        ),
    )(queries, keys, values, out_cotangent)
    return pl.pallas_call(
        finish,
        out_shape=(
            jax.ShapeDtypeStruct((BLOCK, DH), F32),
            jax.ShapeDtypeStruct(keys.shape, BF16),
            jax.ShapeDtypeStruct(values.shape, BF16),
        ),
        in_specs=[pl.BlockSpec(memory_space=pltpu.VMEM)] * 3,
        out_specs=(pl.BlockSpec(memory_space=pltpu.VMEM), anywhere, anywhere),
        scratch_shapes=[dma((2,))],
        compiler_params=pltpu.CompilerParams(vmem_limit_bytes=4 * 2**20),
    )(parts, key_gradient, value_gradient)


def solution(mesh):
    placed = (P("mp", None), P("dp", "mp", None), P("dp", "mp", None), P("dp", "mp", None))
    return jax.shard_map(
        on_device,
        mesh=mesh,
        in_specs=placed,
        out_specs=(P("mp", None), P("dp", "mp", None), P("dp", "mp", None)),
        check_vma=False,
    )
```

```python
import math

import jax
import jax.numpy as jnp
from jax import lax
from jax.experimental import pallas as pl
from jax.experimental.pallas import tpu as pltpu
from jax.sharding import PartitionSpec as P

HEADS = 16
DH = 256
R = 768
DOCS = 4
MP = 64
CORES = 2
Z = 8
OWNERS = Z // 2
K = MP // Z
BLOCK = 192
HALF = BLOCK // 2
POS = 64
HERE = K * POS
WIDE = 2 * BLOCK
SCALE = 1.0 / math.sqrt(DH)
MESH = pl.DeviceIdType.MESH
F32 = jnp.float32
BF16 = jnp.bfloat16


def dot(a, b, dims):
    return lax.dot_general(a, b, (dims, ((), ())), preferred_element_type=F32)


def kernel(
    q_in, k_in, v_in, g_in,
    yrecv, dk_out, dv_out,
    kbuf, vbuf, qbuf, gbuf, pbuf, wbuf, p16, s16, aq, bq, dkst, dvst,
    zsend, zrecv, mstat, tstat, logs, deltas,
    own_sem, ksem, vsem, rsend, rrecv, gsem, lsem, dsem, dksem, dvsem, zsem, zown, ysem,
):
    dp, mp = lax.axis_index("dp"), lax.axis_index("mp")
    k, z = lax.div(mp, Z), lax.rem(mp, Z)
    core = lax.rem(dp, CORES)
    first_core = dp - core
    sibling = first_core + 1 - core
    home = lax.div(z, OWNERS)
    right = k * Z + lax.rem(z + 1, Z)
    left = k * Z + lax.rem(z + Z - 1, Z)

    def remote(src, dst, ssem, rsem, where):
        return pltpu.make_async_remote_copy(
            src_ref=src, dst_ref=dst, send_sem=ssem, recv_sem=rsem, device_id=where, device_id_type=MESH
        )

    def mate(d):
        j = lax.rem(k + d, K)
        return j, j * Z + z

    def ringmate(d):
        return dp, k * Z + lax.rem(z + d, Z)

    def doc(d):
        return lax.rem(dp + d, DOCS), mp

    barrier = pltpu.get_barrier_semaphore()
    partners = [(first_core + c, mate(d)[1]) for d in range(1, K) for c in range(CORES)]
    partners += [(sibling, right), (sibling, left)]
    partners += [ringmate(d) for d in range(1, Z)]
    partners += [doc(d) for d in range(1, DOCS)]
    for where in partners:
        pl.semaphore_signal(barrier, inc=1, device_id=where, device_id_type=MESH)
    pl.semaphore_wait(barrier, len(partners))

    def pos_of(j, which=0):
        return pl.ds(pl.multiple_of(which * HERE + j * POS, POS), POS)

    def cols_of(j, which):
        return pl.ds(pl.multiple_of((j * CORES + which) * DH, DH), DH)

    def piece(part, j, h, side):
        start = lax.rem(j, OWNERS) * BLOCK + (side * HALF if h == 3 else 0)
        size = HALF if h == 3 else BLOCK
        if part == 0:
            return qbuf.at[pl.ds(pl.multiple_of(start, 32), size)]
        return gbuf.at[pl.ds(pl.multiple_of((part - 1) * R + start, 32), size)]

    def own_cotangent():
        return gbuf.at[pl.ds(pl.multiple_of(core * R + lax.rem(z, OWNERS) * BLOCK, 32), BLOCK)]

    def slot(part, h, side):
        return (part * 2 + side) * 4 + h

    def hop(part, h, side):
        j = lax.rem(z + (Z - h if side == 0 else h), Z)
        there = piece(part, j, h, side)
        src = q_in if h == 0 else there
        i = slot(part, h, side)
        return remote(src, there, rsend.at[i], rrecv.at[i], (dp, right if side == 0 else left))

    def arrival(part, h, side):
        j = lax.rem(z + (Z - 1 - h if side == 0 else h + 1), Z)
        there = piece(part, j, h, side)
        i = slot(part, h, side)
        return remote(there, there, rsend.at[i], rrecv.at[i], (dp, right if side == 0 else left))

    def concerns(h, side):
        j = lax.rem(z + (Z - 1 - h if side == 0 else h + 1), Z)
        return lax.div(j, OWNERS) == core

    def cotangent_hop(side):
        where = (first_core + home, right if side == 0 else left)
        return remote(g_in.at[0], own_cotangent(), gsem.at[side], rrecv.at[4 * side + 8 + 8 * core], where)

    def cotangent_share():
        return remote(g_in.at[0], own_cotangent(), gsem.at[2], gsem.at[3], (sibling, mp))

    @pl.when(core == home)
    def _():
        for side in range(2):
            hop(0, 0, side).start()

    for side in range(2):
        cotangent_hop(side).start()

    @pl.when(core != home)
    def _():
        cotangent_share().start()

    def spread(src, buf, sem):
        for d in range(1, K):
            j, there = mate(d)
            for c in range(CORES):
                where = (first_core + c, there)
                remote(src.at[0, :, cols_of(j, c)], buf.at[pos_of(k, core)], sem.at[0], sem.at[1], where).start()
        where = (sibling, mp)
        remote(src.at[0, :, cols_of(k, 1 - core)], buf.at[pos_of(k, core)], sem.at[0], sem.at[1], where).start()

    spread(k_in, kbuf, ksem)
    spread(v_in, vbuf, vsem)

    own = [
        pltpu.make_async_copy(k_in.at[0, :, cols_of(k, core)], kbuf.at[pos_of(k, core)], own_sem.at[2]),
        pltpu.make_async_copy(v_in.at[0, :, cols_of(k, core)], vbuf.at[pos_of(k, core)], own_sem.at[3]),
    ]
    own_block = [
        pltpu.make_async_copy(q_in, piece(0, z, 0, 0), own_sem.at[0]),
        pltpu.make_async_copy(g_in.at[0], own_cotangent(), own_sem.at[1]),
    ]
    for copy in own:
        copy.start()

    @pl.when(core == home)
    def _():
        for copy in own_block:
            copy.start()

    for h in range(1, 4):
        for part in range(3):
            for side in range(2):

                @pl.when(concerns(h - 1, side))
                def _(h=h, part=part, side=side):
                    arrival(part, h - 1, side).wait_recv()
                    hop(part, h, side).start()

    def all_mates(buf, sem):
        there = buf.at[pl.ds(0, (CORES * K - 1) * POS)]
        return remote(there, there, sem.at[0], sem.at[1], (sibling, mp))

    def place(d, w):
        rows = pl.ds(pl.multiple_of(w * WIDE, WIDE), WIDE)
        cotangents = pl.ds(pl.multiple_of(d * R + w * WIDE, WIDE), WIDE)
        return d * 2 + w, pl.ds(d * HERE, HERE), rows, cotangents

    def score(d, w):
        i, docs, rows, _ = place(d, w)
        s = dot(kbuf[docs, :], qbuf[rows, :], ((1,), (1,))) * SCALE
        top = jnp.max(s, axis=0, keepdims=True)
        p = jnp.exp(s - top)
        total = jnp.sum(p, axis=0, keepdims=True)
        pbuf[i] = p
        p16[d, :, rows] = p.astype(BF16)
        mstat[d, :, rows] = top
        tstat[d, :, rows] = total
        logs[z, d, :, rows] = top + jnp.log(total)

    def weigh(d, w):
        i, docs, rows, cotangents = place(d, w)
        c = dot(vbuf[docs, :], gbuf[cotangents, :], ((1,), (1,)))
        wbuf[i] = c
        deltas[z, d, :, rows] = jnp.sum(pbuf[i] * c, axis=0, keepdims=True) / tstat[d, :, rows]

    def settle(d, w):
        i, _, rows, _ = place(d, w)
        s16[d, :, rows] = (pbuf[i] * (wbuf[i] - deltas[z, d, :, rows])).astype(BF16)

    late = lax.div(lax.rem(z, OWNERS), 2)
    early = 1 - late
    for copy in own:
        copy.wait()

    @pl.when(core == home)
    def _():
        for copy in own_block:
            copy.wait()
        cotangent_share().wait_recv()

    all_mates(kbuf, ksem).wait_recv()
    for d in range(CORES):
        score(d, early)
    all_mates(vbuf, vsem).wait_recv()
    for d in range(CORES):
        weigh(d, early)
        settle(d, early)

    def last(part):
        @pl.when(core != home)
        def _():
            for side in range(2):
                arrival(part, 3, side).wait_recv()

    def tell(stat, sem):
        for d in (4, 3, 5, 2, 6, 1, 7):
            remote(stat.at[z], stat.at[z], sem.at[0], sem.at[1], ringmate(d)).start()

    def told(stat, sem):
        there = stat.at[pl.ds(0, Z - 1)]
        return remote(there, there, sem.at[0], sem.at[1], ringmate(1))

    last(0)
    for d in range(CORES):
        score(d, late)
    tell(logs, lsem)
    for d in range(CORES):
        last(1 + d)
        weigh(d, late)
    tell(deltas, dsem)
    for d in range(CORES):
        docs = pl.ds(d * HERE, HERE)
        settle(d, late)
        aq[d] = dot(s16[d], kbuf[docs, :], ((0,), (0,)))
        bq[d] = dot(p16[d], kbuf[docs, :], ((0,), (0,)))

    def columns(rows):
        return jnp.concatenate(rows + [jnp.zeros((8 - len(rows), R), F32)], axis=0).T

    def back(stage, out, sem, values_of):
        for d in range(CORES):
            stage[d * HERE : (d + 1) * HERE, :] = values_of(d).astype(BF16)
        there = out.at[0, :, cols_of(k, core)]
        for e in range(1, K):
            j, to = mate(e)
            for d in range(CORES):
                remote(stage.at[pos_of(j, d)], there, sem.at[0], sem.at[1], (first_core + d, to)).start()
        remote(stage.at[pos_of(k, 1 - core)], there, sem.at[0], sem.at[1], (sibling, mp)).start()

    told(logs, lsem).wait_recv()
    weights, factors = [], []
    for d in range(CORES):
        parts = [logs[j, d] for j in range(Z)]
        peak = parts[0]
        for part in parts[1:]:
            peak = jnp.maximum(peak, part)
        shares = [jnp.exp(part - peak) for part in parts]
        whole = shares[0]
        for part in shares[1:]:
            whole = whole + part
        weights.append([share / whole for share in shares])
        factors.append(jnp.exp(mstat[d] - (peak + jnp.log(whole))))
    factor = columns(factors)

    def value_part(d):
        rows = gbuf[d * R : (d + 1) * R, :].astype(F32) * factor[:, d : d + 1]
        return dot(p16[d], rows.astype(BF16), ((1,), (0,)))

    back(dvst, dv_out, dvsem, value_part)

    told(deltas, dsem).wait_recv()
    changes = []
    for d in range(CORES):
        delta = weights[d][0] * deltas[0, d]
        for j in range(1, Z):
            delta = delta + weights[d][j] * deltas[j, d]
        changes.append(factors[d] * (deltas[z, d] - delta))
    change = columns(changes)

    def z_copy(b, c):
        src = zsend.at[b, pl.ds(c * HALF, HALF)]
        where = (first_core + c, k * Z + core * OWNERS + b)
        return remote(src, zrecv.at[z], zsem.at[0], zsem.at[1], where)

    def z_own():
        src = zsend.at[lax.rem(z, OWNERS), pl.ds(pl.multiple_of((1 - core) * HALF, HALF), HALF)]
        return remote(src, zrecv.at[z], zown.at[0], zown.at[1], (sibling, mp))

    for b in range(OWNERS):
        rows = slice(b * BLOCK, (b + 1) * BLOCK)
        part = factor[rows, 0:1] * aq[0, rows, :] + change[rows, 0:1] * bq[0, rows, :]
        part = part + factor[rows, 1:2] * aq[1, rows, :] + change[rows, 1:2] * bq[1, rows, :]
        zsend[b] = (part * SCALE).astype(BF16)

        @pl.when(core * OWNERS + b != z)
        def _(b=b):
            for c in range(CORES):
                z_copy(b, c).start()

    @pl.when(core == home)
    def _():
        z_own().start()
        mine = pl.ds(pl.multiple_of(core * HALF, HALF), HALF)
        zrecv[z] = zsend[lax.rem(z, OWNERS), mine, :]

    def key_part(d):
        rows = qbuf[...].astype(F32)
        main = (rows * (factor[:, d : d + 1] * SCALE)).astype(BF16)
        rest = (rows * (change[:, d : d + 1] * SCALE)).astype(BF16)
        return dot(s16[d], main, ((1,), (0,))) + dot(p16[d], rest, ((1,), (0,)))

    back(dkst, dk_out, dksem, key_part)
    kept = [
        pltpu.make_async_copy(dvst.at[pos_of(k, core)], dv_out.at[0, :, cols_of(k, core)], own_sem.at[0]),
        pltpu.make_async_copy(dkst.at[pos_of(k, core)], dk_out.at[0, :, cols_of(k, core)], own_sem.at[1]),
    ]
    for copy in kept:
        copy.start()

    @pl.when(core == home)
    def _():
        for side in range(2):
            hop(0, 0, side).wait_send()

    for side in range(2):
        cotangent_hop(side).wait_send()

    @pl.when(core != home)
    def _():
        cotangent_share().wait_send()

    for h in range(1, 4):
        for side in range(2):

            @pl.when(concerns(h - 1, side))
            def _(h=h, side=side):
                for part in range(3):
                    hop(part, h, side).wait_send()

    all_mates(kbuf, ksem).wait_send()
    all_mates(vbuf, vsem).wait_send()
    told(logs, lsem).wait_send()
    told(deltas, dsem).wait_send()

    @pl.when(core != home)
    def _():
        z_own().wait_recv()

    pieces = zrecv.at[pl.ds(0, Z - 1)]
    remote(pieces, pieces, zsem.at[0], zsem.at[1], ringmate(1)).wait_recv()
    half_sum = zrecv[0].astype(F32)
    for j in range(1, Z):
        half_sum = half_sum + zrecv[j].astype(F32)
    yrecv[dp] = half_sum.astype(BF16)

    for d in range(1, DOCS):
        remote(yrecv.at[dp], yrecv.at[dp], ysem.at[0], ysem.at[1], doc(d)).start()

    def all_docs():
        there = yrecv.at[pl.ds(0, DOCS - 1)]
        return remote(there, there, ysem.at[0], ysem.at[1], doc(1))

    all_docs().wait_recv()
    for copy in kept:
        copy.wait()
    for out, sem in ((dv_out, dvsem), (dk_out, dksem)):
        there = out.at[0, :, pl.ds(0, (CORES * K - 1) * DH)]
        done = remote(there, there, sem.at[0], sem.at[1], (sibling, mp))
        done.wait_send()
        done.wait_recv()

    @pl.when(core == home)
    def _():
        z_own().wait_send()

    for b in range(OWNERS):

        @pl.when(core * OWNERS + b != z)
        def _(b=b):
            for c in range(CORES):
                z_copy(b, c).wait_send()

    all_docs().wait_send()


def finish(parts, dk_in, dv_in, dq_out, dk_out, dv_out, sem):
    copies = [
        pltpu.make_async_copy(dk_in, dk_out, sem.at[0]),
        pltpu.make_async_copy(dv_in, dv_out, sem.at[1]),
    ]
    for copy in copies:
        copy.start()
    for h in range(2):
        dq_out[pl.ds(h * HALF, HALF), :] = parts[h].astype(F32) + parts[2 + h].astype(F32)
    for copy in copies:
        copy.wait()


def on_device(queries, keys, values, out_cotangent):
    queries, keys, values, out_cotangent = (
        pltpu.with_memory_space_constraint(x, pltpu.HBM) for x in (queries, keys, values, out_cotangent)
    )
    anywhere = pl.BlockSpec(memory_space=pl.ANY)
    inside = pl.BlockSpec(memory_space=pltpu.VMEM)
    dma = pltpu.SemaphoreType.DMA
    parts, key_gradient, value_gradient = pl.pallas_call(
        kernel,
        out_shape=(
            pltpu.VMEM((DOCS, HALF, DH), BF16),
            pltpu.VMEM(keys.shape, BF16),
            pltpu.VMEM(values.shape, BF16),
        ),
        in_specs=[anywhere] * 4,
        out_specs=[inside] * 3,
        scratch_shapes=[
            pltpu.VMEM((CORES * HERE, DH), BF16),
            pltpu.VMEM((CORES * HERE, DH), BF16),
            pltpu.VMEM((R, DH), BF16),
            pltpu.VMEM((CORES * R, DH), BF16),
            pltpu.VMEM((2 * CORES, HERE, WIDE), F32),
            pltpu.VMEM((2 * CORES, HERE, WIDE), F32),
            pltpu.VMEM((CORES, HERE, R), BF16),
            pltpu.VMEM((CORES, HERE, R), BF16),
            pltpu.VMEM((CORES, R, DH), F32),
            pltpu.VMEM((CORES, R, DH), F32),
            pltpu.VMEM((CORES * HERE, DH), BF16),
            pltpu.VMEM((CORES * HERE, DH), BF16),
            pltpu.VMEM((OWNERS, BLOCK, DH), BF16),
            pltpu.VMEM((Z, HALF, DH), BF16),
            pltpu.VMEM((CORES, 1, R), F32),
            pltpu.VMEM((CORES, 1, R), F32),
            pltpu.VMEM((Z, CORES, 1, R), F32),
            pltpu.VMEM((Z, CORES, 1, R), F32),
            dma((4,)), dma((2,)), dma((2,)), dma((24,)), dma((24,)), dma((4,)), dma((2,)), dma((2,)),
            dma((2,)), dma((2,)), dma((2,)), dma((2,)), dma((2,)),
        ],
        compiler_params=pltpu.CompilerParams(
            collective_id=0, has_side_effects=True, vmem_limit_bytes=48 * 2**20
        ),
        cost_estimate=pl.CostEstimate(
            flops=10 * HERE * CORES * R * DH, bytes_accessed=4 * 2**20, transcendentals=HERE * CORES * R
        ),
    )(queries, keys, values, out_cotangent)
    return pl.pallas_call(
        finish,
        out_shape=(
            jax.ShapeDtypeStruct((BLOCK, DH), F32),
            jax.ShapeDtypeStruct(keys.shape, BF16),
            jax.ShapeDtypeStruct(values.shape, BF16),
        ),
        in_specs=[inside] * 3,
        out_specs=(inside, anywhere, anywhere),
        scratch_shapes=[dma((2,))],
        compiler_params=pltpu.CompilerParams(vmem_limit_bytes=4 * 2**20),
    )(parts, key_gradient, value_gradient)


def solution(mesh):
    placed = (P("mp", None), P("dp", "mp", None), P("dp", "mp", None), P("dp", "mp", None))
    return jax.shard_map(
        on_device,
        mesh=mesh,
        in_specs=placed,
        out_specs=(P("mp", None), P("dp", "mp", None), P("dp", "mp", None)),
        check_vma=False,
    )
```

```python
import math

import jax
import jax.numpy as jnp
from jax import lax
from jax.experimental import pallas as pl
from jax.experimental.pallas import tpu as pltpu
from jax.sharding import PartitionSpec as P

HEADS = 16
DH = 256
R = 768
DOCS = 4
MP = 64
CORES = 2
Z = 8
OWNERS = Z // 2
K = MP // Z
BLOCK = 192
HALF = BLOCK // 2
POS = 64
HERE = K * POS
WIDE = 2 * BLOCK
SCALE = 1.0 / math.sqrt(DH)
MESH = pl.DeviceIdType.MESH
F32 = jnp.float32
BF16 = jnp.bfloat16


def dot(a, b, dims):
    return lax.dot_general(a, b, (dims, ((), ())), preferred_element_type=F32)


def kernel(
    q_in, k_in, v_in, g_in,
    yrecv, dk_out, dv_out,
    kown, vown, gown, kbuf, vbuf, qbuf, gbuf, pbuf, wbuf, p16, s16, aq, bq, dkst, dvst,
    zsend, zrecv, mstat, tstat, logs, deltas,
    own_sem, ksem, vsem, rsend, rrecv, gsem, lsem, dsem, dksem, dvsem, zsem, zown, ysem,
):
    dp, mp = lax.axis_index("dp"), lax.axis_index("mp")
    k, z = lax.div(mp, Z), lax.rem(mp, Z)
    core = lax.rem(dp, CORES)
    first_core = dp - core
    sibling = first_core + 1 - core
    home = lax.div(z, OWNERS)
    right = k * Z + lax.rem(z + 1, Z)
    left = k * Z + lax.rem(z + Z - 1, Z)

    def remote(src, dst, ssem, rsem, where):
        return pltpu.make_async_remote_copy(
            src_ref=src, dst_ref=dst, send_sem=ssem, recv_sem=rsem, device_id=where, device_id_type=MESH
        )

    def mate(d):
        j = lax.rem(k + d, K)
        return j, j * Z + z

    def ringmate(d):
        return dp, k * Z + lax.rem(z + d, Z)

    def doc(d):
        return lax.rem(dp + d, DOCS), mp

    barrier = pltpu.get_barrier_semaphore()
    partners = [(first_core + c, mate(d)[1]) for d in range(1, K) for c in range(CORES)]
    partners += [(sibling, right), (sibling, left)]
    partners += [ringmate(d) for d in range(1, Z)]
    partners += [doc(d) for d in range(1, DOCS)]
    for where in partners:
        pl.semaphore_signal(barrier, inc=1, device_id=where, device_id_type=MESH)

    def pos_of(j, which=0):
        return pl.ds(pl.multiple_of(which * HERE + j * POS, POS), POS)

    def cols_of(j, which):
        return pl.ds(pl.multiple_of((j * CORES + which) * DH, DH), DH)

    def piece(part, j, h, side):
        start = lax.rem(j, OWNERS) * BLOCK + (side * HALF if h == 3 else 0)
        size = HALF if h == 3 else BLOCK
        if part == 0:
            return qbuf.at[pl.ds(pl.multiple_of(start, 32), size)]
        return gbuf.at[pl.ds(pl.multiple_of((part - 1) * R + start, 32), size)]

    def own_queries():
        return qbuf.at[pl.ds(pl.multiple_of(lax.rem(z, OWNERS) * BLOCK, 32), BLOCK)]

    def own_cotangent():
        return gbuf.at[pl.ds(pl.multiple_of(core * R + lax.rem(z, OWNERS) * BLOCK, 32), BLOCK)]

    def slot(part, h, side):
        return (part * 2 + side) * 4 + h

    def hop(part, h, side):
        j = lax.rem(z + (Z - h if side == 0 else h), Z)
        there = piece(part, j, h, side)
        src = own_queries() if h == 0 else there
        i = slot(part, h, side)
        return remote(src, there, rsend.at[i], rrecv.at[i], (dp, right if side == 0 else left))

    def arrival(part, h, side):
        j = lax.rem(z + (Z - 1 - h if side == 0 else h + 1), Z)
        there = piece(part, j, h, side)
        i = slot(part, h, side)
        return remote(there, there, rsend.at[i], rrecv.at[i], (dp, right if side == 0 else left))

    def concerns(h, side):
        j = lax.rem(z + (Z - 1 - h if side == 0 else h + 1), Z)
        return lax.div(j, OWNERS) == core

    def cotangent_hop(side):
        where = (first_core + home, right if side == 0 else left)
        return remote(gown, own_cotangent(), gsem.at[side], rrecv.at[4 * side + 8 + 8 * core], where)

    def cotangent_share():
        return remote(gown, own_cotangent(), gsem.at[2], gsem.at[3], (sibling, mp))

    staged = [
        pltpu.make_async_copy(q_in, own_queries(), own_sem.at[0]),
        pltpu.make_async_copy(g_in.at[0], gown, own_sem.at[1]),
        pltpu.make_async_copy(k_in.at[0], kown, own_sem.at[2]),
        pltpu.make_async_copy(v_in.at[0], vown, own_sem.at[3]),
    ]
    own = [
        pltpu.make_async_copy(gown, own_cotangent(), own_sem.at[1]),
        pltpu.make_async_copy(kown.at[:, cols_of(k, core)], kbuf.at[pos_of(k, core)], own_sem.at[2]),
        pltpu.make_async_copy(vown.at[:, cols_of(k, core)], vbuf.at[pos_of(k, core)], own_sem.at[3]),
    ]

    for copy in staged[1:]:
        copy.start()

    @pl.when(core == home)
    def _():
        staged[0].start()
        staged[0].wait()

    for copy in staged[1:]:
        copy.wait()
    pl.semaphore_wait(barrier, len(partners))

    @pl.when(core == home)
    def _():
        for side in range(2):
            hop(0, 0, side).start()

    for side in range(2):
        cotangent_hop(side).start()

    @pl.when(core != home)
    def _():
        cotangent_share().start()

    def spread(src, buf, sem):
        for other in range(CORES):
            c = lax.rem(core + other, CORES)

            @pl.loop(1, K)
            def _(d):
                j, there = mate(d)
                where = (first_core + c, there)
                remote(src.at[:, cols_of(j, c)], buf.at[pos_of(k, core)], sem.at[0], sem.at[1], where).start()

        where = (sibling, mp)
        remote(src.at[:, cols_of(k, 1 - core)], buf.at[pos_of(k, core)], sem.at[0], sem.at[1], where).start()

    spread(kown, kbuf, ksem)
    spread(vown, vbuf, vsem)
    for copy in own[1:]:
        copy.start()

    @pl.when(core == home)
    def _():
        own[0].start()


    for h in range(1, 4):
        for part in range(3):
            for side in range(2):

                @pl.when(concerns(h - 1, side))
                def _(h=h, part=part, side=side):
                    arrival(part, h - 1, side).wait_recv()
                    hop(part, h, side).start()

    def all_mates(buf, sem):
        there = buf.at[pl.ds(0, (CORES * K - 1) * POS)]
        return remote(there, there, sem.at[0], sem.at[1], (sibling, mp))

    def place(d, w):
        rows = pl.ds(pl.multiple_of(w * WIDE, WIDE), WIDE)
        cotangents = pl.ds(pl.multiple_of(d * R + w * WIDE, WIDE), WIDE)
        return d * 2 + w, pl.ds(d * HERE, HERE), rows, cotangents

    def score(d, w):
        i, docs, rows, _ = place(d, w)
        s = dot(kbuf[docs, :], qbuf[rows, :], ((1,), (1,))) * SCALE
        top = jnp.max(s, axis=0, keepdims=True)
        p = jnp.exp(s - top)
        total = jnp.sum(p, axis=0, keepdims=True)
        pbuf[i] = p
        p16[d, :, rows] = p.astype(BF16)
        mstat[d, :, rows] = top
        tstat[d, :, rows] = total
        logs[z, d, :, rows] = top + jnp.log(total)

    def weigh(d, w):
        i, docs, rows, cotangents = place(d, w)
        c = dot(vbuf[docs, :], gbuf[cotangents, :], ((1,), (1,)))
        wbuf[i] = c
        deltas[z, d, :, rows] = jnp.sum(pbuf[i] * c, axis=0, keepdims=True) / tstat[d, :, rows]

    def settle(d, w):
        i, _, rows, _ = place(d, w)
        s16[d, :, rows] = (pbuf[i] * (wbuf[i] - deltas[z, d, :, rows])).astype(BF16)

    late = lax.div(lax.rem(z, OWNERS), 2)
    early = 1 - late
    for copy in own[1:]:
        copy.wait()

    @pl.when(core == home)
    def _():
        own[0].wait()
        cotangent_share().wait_recv()

    all_mates(kbuf, ksem).wait_recv()
    for d in range(CORES):
        score(d, early)
    all_mates(vbuf, vsem).wait_recv()
    for d in range(CORES):
        weigh(d, early)
        settle(d, early)

    def last(part):
        @pl.when(core != home)
        def _():
            for side in range(2):
                arrival(part, 3, side).wait_recv()

    def tell(stat, sem):
        for d in (4, 3, 5, 2, 6, 1, 7):
            remote(stat.at[z], stat.at[z], sem.at[0], sem.at[1], ringmate(d)).start()

    def told(stat, sem):
        there = stat.at[pl.ds(0, Z - 1)]
        return remote(there, there, sem.at[0], sem.at[1], ringmate(1))

    last(0)
    for d in range(CORES):
        score(d, late)
    tell(logs, lsem)
    for d in range(CORES):
        last(1 + d)
        weigh(d, late)
    tell(deltas, dsem)
    for d in range(CORES):
        docs = pl.ds(d * HERE, HERE)
        settle(d, late)
        aq[d] = dot(s16[d], kbuf[docs, :], ((0,), (0,)))
        bq[d] = dot(p16[d], kbuf[docs, :], ((0,), (0,)))

    def columns(rows):
        return jnp.concatenate(rows + [jnp.zeros((8 - len(rows), R), F32)], axis=0).T

    def back(stage, out, sem, d, values):
        stage[d * HERE : (d + 1) * HERE, :] = values.astype(BF16)
        there = out.at[0, :, cols_of(k, core)]

        @pl.loop(1, K)
        def _(e):
            j, to = mate(e)
            remote(stage.at[pos_of(j, d)], there, sem.at[0], sem.at[1], (first_core + d, to)).start()

        @pl.when(core != d)
        def _():
            remote(stage.at[pos_of(k, d)], there, sem.at[0], sem.at[1], (sibling, mp)).start()

    told(logs, lsem).wait_recv()
    weights, factors = [], []
    for d in range(CORES):
        parts = [logs[j, d] for j in range(Z)]
        peak = parts[0]
        for part in parts[1:]:
            peak = jnp.maximum(peak, part)
        shares = [jnp.exp(part - peak) for part in parts]
        whole = shares[0]
        for part in shares[1:]:
            whole = whole + part
        weights.append([share / whole for share in shares])
        factors.append(jnp.exp(mstat[d] - (peak + jnp.log(whole))))
    factor = columns(factors)

    def value_part(d):
        rows = gbuf[d * R : (d + 1) * R, :].astype(F32) * factor[:, d : d + 1]
        return dot(p16[d], rows.astype(BF16), ((1,), (0,)))

    back(dvst, dv_out, dvsem, 0, value_part(0))

    aq[0] = factor[:, 0:1] * aq[0] + factor[:, 1:2] * aq[1]

    told(deltas, dsem).wait_recv()
    changes = []
    for d in range(CORES):
        delta = weights[d][0] * deltas[0, d]
        for j in range(1, Z):
            delta = delta + weights[d][j] * deltas[j, d]
        changes.append(factors[d] * (deltas[z, d] - delta))
    change = columns(changes)

    def z_copy(b, c):
        src = zsend.at[b, pl.ds(c * HALF, HALF)]
        where = (first_core + c, k * Z + core * OWNERS + b)
        return remote(src, zrecv.at[z], zsem.at[0], zsem.at[1], where)

    def z_own():
        src = zsend.at[lax.rem(z, OWNERS), pl.ds(pl.multiple_of((1 - core) * HALF, HALF), HALF)]
        return remote(src, zrecv.at[z], zown.at[0], zown.at[1], (sibling, mp))

    for b in range(OWNERS):
        rows = slice(b * BLOCK, (b + 1) * BLOCK)
        part = aq[0, rows, :] + change[rows, 0:1] * bq[0, rows, :] + change[rows, 1:2] * bq[1, rows, :]
        zsend[b] = (part * SCALE).astype(BF16)

        @pl.when(core * OWNERS + b != z)
        def _(b=b):
            for c in range(CORES):
                z_copy(b, c).start()

    @pl.when(core == home)
    def _():
        z_own().start()
        mine = pl.ds(pl.multiple_of(core * HALF, HALF), HALF)
        zrecv[z] = zsend[lax.rem(z, OWNERS), mine, :]

    def key_part(d):
        rows = qbuf[...].astype(F32)
        main = (rows * (factor[:, d : d + 1] * SCALE)).astype(BF16)
        rest = (rows * (change[:, d : d + 1] * SCALE)).astype(BF16)
        return dot(s16[d], main, ((1,), (0,))) + dot(p16[d], rest, ((1,), (0,)))

    back(dvst, dv_out, dvsem, 1, value_part(1))
    for d in range(CORES):
        back(dkst, dk_out, dksem, d, key_part(d))
    kept = [
        pltpu.make_async_copy(dvst.at[pos_of(k, core)], dv_out.at[0, :, cols_of(k, core)], own_sem.at[0]),
        pltpu.make_async_copy(dkst.at[pos_of(k, core)], dk_out.at[0, :, cols_of(k, core)], own_sem.at[1]),
    ]
    for copy in kept:
        copy.start()

    @pl.when(core == home)
    def _():
        for side in range(2):
            hop(0, 0, side).wait_send()

    for side in range(2):
        cotangent_hop(side).wait_send()

    @pl.when(core != home)
    def _():
        cotangent_share().wait_send()

    for h in range(1, 4):
        for side in range(2):

            @pl.when(concerns(h - 1, side))
            def _(h=h, side=side):
                for part in range(3):
                    hop(part, h, side).wait_send()

    all_mates(kbuf, ksem).wait_send()
    all_mates(vbuf, vsem).wait_send()
    told(logs, lsem).wait_send()
    told(deltas, dsem).wait_send()

    @pl.when(core != home)
    def _():
        z_own().wait_recv()

    pieces = zrecv.at[pl.ds(0, Z - 1)]
    remote(pieces, pieces, zsem.at[0], zsem.at[1], ringmate(1)).wait_recv()
    half_sum = zrecv[0].astype(F32)
    for j in range(1, Z):
        half_sum = half_sum + zrecv[j].astype(F32)
    yrecv[dp] = half_sum.astype(BF16)

    for d in range(1, DOCS):
        remote(yrecv.at[dp], yrecv.at[dp], ysem.at[0], ysem.at[1], doc(d)).start()

    def all_docs():
        there = yrecv.at[pl.ds(0, DOCS - 1)]
        return remote(there, there, ysem.at[0], ysem.at[1], doc(1))

    all_docs().wait_recv()
    for copy in kept:
        copy.wait()
    for out, sem in ((dv_out, dvsem), (dk_out, dksem)):
        there = out.at[0, :, pl.ds(0, (CORES * K - 1) * DH)]
        done = remote(there, there, sem.at[0], sem.at[1], (sibling, mp))
        done.wait_send()
        done.wait_recv()

    @pl.when(core == home)
    def _():
        z_own().wait_send()

    for b in range(OWNERS):

        @pl.when(core * OWNERS + b != z)
        def _(b=b):
            for c in range(CORES):
                z_copy(b, c).wait_send()

    all_docs().wait_send()


def finish(parts, dk_in, dv_in, dq_out, dk_out, dv_out, total, sem):
    copies = [
        pltpu.make_async_copy(dk_in, dk_out, sem.at[0]),
        pltpu.make_async_copy(dv_in, dv_out, sem.at[1]),
    ]
    for copy in copies:
        copy.start()
    for h in range(2):
        total[pl.ds(h * HALF, HALF), :] = parts[h].astype(F32) + parts[2 + h].astype(F32)
    copies.append(pltpu.make_async_copy(total, dq_out, sem.at[2]))
    copies[2].start()
    for copy in copies:
        copy.wait()


def on_device(queries, keys, values, out_cotangent):
    queries, keys, values, out_cotangent = (
        pltpu.with_memory_space_constraint(x, pltpu.HBM) for x in (queries, keys, values, out_cotangent)
    )
    anywhere = pl.BlockSpec(memory_space=pl.ANY)
    inside = pl.BlockSpec(memory_space=pltpu.VMEM)
    dma = pltpu.SemaphoreType.DMA
    parts, key_gradient, value_gradient = pl.pallas_call(
        kernel,
        out_shape=(
            pltpu.VMEM((DOCS, HALF, DH), BF16),
            pltpu.VMEM(keys.shape, BF16),
            pltpu.VMEM(values.shape, BF16),
        ),
        in_specs=[anywhere] * 4,
        out_specs=[inside] * 3,
        scratch_shapes=[
            pltpu.VMEM((POS, HEADS * DH), BF16),
            pltpu.VMEM((POS, HEADS * DH), BF16),
            pltpu.VMEM((BLOCK, DH), BF16),
            pltpu.VMEM((CORES * HERE, DH), BF16),
            pltpu.VMEM((CORES * HERE, DH), BF16),
            pltpu.VMEM((R, DH), BF16),
            pltpu.VMEM((CORES * R, DH), BF16),
            pltpu.VMEM((2 * CORES, HERE, WIDE), F32),
            pltpu.VMEM((2 * CORES, HERE, WIDE), F32),
            pltpu.VMEM((CORES, HERE, R), BF16),
            pltpu.VMEM((CORES, HERE, R), BF16),
            pltpu.VMEM((CORES, R, DH), F32),
            pltpu.VMEM((CORES, R, DH), F32),
            pltpu.VMEM((CORES * HERE, DH), BF16),
            pltpu.VMEM((CORES * HERE, DH), BF16),
            pltpu.VMEM((OWNERS, BLOCK, DH), BF16),
            pltpu.VMEM((Z, HALF, DH), BF16),
            pltpu.VMEM((CORES, 1, R), F32),
            pltpu.VMEM((CORES, 1, R), F32),
            pltpu.VMEM((Z, CORES, 1, R), F32),
            pltpu.VMEM((Z, CORES, 1, R), F32),
            dma((4,)), dma((2,)), dma((2,)), dma((24,)), dma((24,)), dma((4,)), dma((2,)), dma((2,)),
            dma((2,)), dma((2,)), dma((2,)), dma((2,)), dma((2,)),
        ],
        compiler_params=pltpu.CompilerParams(
            collective_id=0, has_side_effects=True, vmem_limit_bytes=48 * 2**20
        ),
        cost_estimate=pl.CostEstimate(
            flops=10 * HERE * CORES * R * DH, bytes_accessed=4 * 2**20, transcendentals=HERE * CORES * R
        ),
    )(queries, keys, values, out_cotangent)
    return pl.pallas_call(
        finish,
        out_shape=(
            jax.ShapeDtypeStruct((BLOCK, DH), F32),
            jax.ShapeDtypeStruct(keys.shape, BF16),
            jax.ShapeDtypeStruct(values.shape, BF16),
        ),
        in_specs=[inside] * 3,
        out_specs=[anywhere] * 3,
        scratch_shapes=[pltpu.VMEM((BLOCK, DH), F32), dma((3,))],
        compiler_params=pltpu.CompilerParams(vmem_limit_bytes=4 * 2**20),
    )(parts, key_gradient, value_gradient)


def solution(mesh):
    placed = (P("mp", None), P("dp", "mp", None), P("dp", "mp", None), P("dp", "mp", None))
    return jax.shard_map(
        on_device,
        mesh=mesh,
        in_specs=placed,
        out_specs=(P("mp", None), P("dp", "mp", None), P("dp", "mp", None)),
        check_vma=False,
    )
```

```python
import math

import jax
import jax.numpy as jnp
from jax import lax
from jax.experimental import pallas as pl
from jax.experimental.pallas import tpu as pltpu
from jax.sharding import PartitionSpec as P

HEADS = 16
DH = 256
R = 768
DOCS = 4
MP = 64
CORES = 2
Z = 8
OWNERS = Z // 2
K = MP // Z
BLOCK = 192
HALF = BLOCK // 2
POS = 64
HERE = K * POS
WIDE = 2 * BLOCK
SCALE = 1.0 / math.sqrt(DH)
MESH = pl.DeviceIdType.MESH
F32 = jnp.float32
BF16 = jnp.bfloat16


def dot(a, b, dims):
    return lax.dot_general(a, b, (dims, ((), ())), preferred_element_type=F32)


def kernel(
    q_in, k_in, v_in, g_in,
    yrecv, dk_out, dv_out,
    kown, vown, gown, kbuf, vbuf, qbuf, gbuf, pbuf, wbuf, p16, s16, aq, bq, dkst, dvst,
    zsend, zrecv, mstat, tstat, logs, deltas,
    own_sem, ksem, vsem, rsend, rrecv, gsem, lsem, dsem, dksem, dvsem, zsem, zown, ysem,
):
    dp, mp = lax.axis_index("dp"), lax.axis_index("mp")
    k, z = lax.div(mp, Z), lax.rem(mp, Z)
    core = lax.rem(dp, CORES)
    first_core = dp - core
    sibling = first_core + 1 - core
    home = lax.div(z, OWNERS)
    right = k * Z + lax.rem(z + 1, Z)
    left = k * Z + lax.rem(z + Z - 1, Z)

    def remote(src, dst, ssem, rsem, where):
        return pltpu.make_async_remote_copy(
            src_ref=src, dst_ref=dst, send_sem=ssem, recv_sem=rsem, device_id=where, device_id_type=MESH
        )

    def mate(d):
        j = lax.rem(k + d, K)
        return j, j * Z + z

    def far_mate(e):
        i, x, y = lax.rem(e, 4), lax.div(k, 2), lax.rem(k, 2)
        dx = 2 + 3 * i + 3 * lax.div(i, 2) + 2 * lax.div(i, 3)
        j = lax.rem(x + dx, 4) * 2 + lax.rem(y + 1 - lax.div(e, 4), 2)
        return j, j * Z + z

    def ringmate(d):
        return dp, k * Z + lax.rem(z + d, Z)

    def doc(d):
        return lax.rem(dp + d, DOCS), mp

    barrier = pltpu.get_barrier_semaphore()
    partners = [(first_core + c, mate(d)[1]) for d in range(1, K) for c in range(CORES)]
    partners += [(sibling, right), (sibling, left)]
    partners += [ringmate(d) for d in range(1, Z)]
    partners += [doc(d) for d in range(1, DOCS)]
    for where in partners:
        pl.semaphore_signal(barrier, inc=1, device_id=where, device_id_type=MESH)

    def pos_of(j, which=0):
        return pl.ds(pl.multiple_of(which * HERE + j * POS, POS), POS)

    def cols_of(j, which):
        return pl.ds(pl.multiple_of((j * CORES + which) * DH, DH), DH)

    def piece(part, j, h, side):
        start = lax.rem(j, OWNERS) * BLOCK + (side * HALF if h == 3 else 0)
        size = HALF if h == 3 else BLOCK
        if part == 0:
            return qbuf.at[pl.ds(pl.multiple_of(start, 32), size)]
        return gbuf.at[pl.ds(pl.multiple_of((part - 1) * R + start, 32), size)]

    def own_queries():
        return qbuf.at[pl.ds(pl.multiple_of(lax.rem(z, OWNERS) * BLOCK, 32), BLOCK)]

    def own_cotangent():
        return gbuf.at[pl.ds(pl.multiple_of(core * R + lax.rem(z, OWNERS) * BLOCK, 32), BLOCK)]

    def slot(part, h, side):
        return (part * 2 + side) * 4 + h

    def hop(part, h, side):
        j = lax.rem(z + (Z - h if side == 0 else h), Z)
        there = piece(part, j, h, side)
        src = own_queries() if h == 0 else there
        i = slot(part, h, side)
        return remote(src, there, rsend.at[i], rrecv.at[i], (dp, right if side == 0 else left))

    def arrival(part, h, side):
        j = lax.rem(z + (Z - 1 - h if side == 0 else h + 1), Z)
        there = piece(part, j, h, side)
        i = slot(part, h, side)
        return remote(there, there, rsend.at[i], rrecv.at[i], (dp, right if side == 0 else left))

    def concerns(h, side):
        j = lax.rem(z + (Z - 1 - h if side == 0 else h + 1), Z)
        return lax.div(j, OWNERS) == core

    def cotangent_hop(side):
        where = (first_core + home, right if side == 0 else left)
        return remote(gown, own_cotangent(), gsem.at[side], rrecv.at[4 * side + 8 + 8 * core], where)

    def cotangent_share():
        return remote(gown, own_cotangent(), gsem.at[2], gsem.at[3], (sibling, mp))

    staged = [
        pltpu.make_async_copy(q_in, own_queries(), own_sem.at[0]),
        pltpu.make_async_copy(g_in.at[0], gown, own_sem.at[1]),
        pltpu.make_async_copy(k_in.at[0], kown, own_sem.at[2]),
        pltpu.make_async_copy(v_in.at[0], vown, own_sem.at[3]),
    ]
    own = [
        pltpu.make_async_copy(gown, own_cotangent(), own_sem.at[1]),
        pltpu.make_async_copy(kown.at[:, cols_of(k, core)], kbuf.at[pos_of(k, core)], own_sem.at[2]),
        pltpu.make_async_copy(vown.at[:, cols_of(k, core)], vbuf.at[pos_of(k, core)], own_sem.at[3]),
    ]

    for copy in staged[1:]:
        copy.start()

    @pl.when(core == home)
    def _():
        staged[0].start()
        staged[0].wait()

    for copy in staged[1:]:
        copy.wait()
    pl.semaphore_wait(barrier, len(partners))

    @pl.when(core == home)
    def _():
        for side in range(2):
            hop(0, 0, side).start()

    for side in range(2):
        cotangent_hop(side).start()

    @pl.when(core != home)
    def _():
        cotangent_share().start()

    def spread(src, buf, sem):
        @pl.loop(0, K - 1)
        def _(e):
            j, there = far_mate(e)
            for c in range(CORES):
                where = (first_core + c, there)
                remote(src.at[:, cols_of(j, c)], buf.at[pos_of(k, core)], sem.at[0], sem.at[1], where).start()


        where = (sibling, mp)
        remote(src.at[:, cols_of(k, 1 - core)], buf.at[pos_of(k, core)], sem.at[0], sem.at[1], where).start()

    spread(kown, kbuf, ksem)
    spread(vown, vbuf, vsem)
    for copy in own[1:]:
        copy.start()

    @pl.when(core == home)
    def _():
        own[0].start()


    for h in range(1, 4):
        for part in range(3):
            for side in range(2):

                @pl.when(concerns(h - 1, side))
                def _(h=h, part=part, side=side):
                    arrival(part, h - 1, side).wait_recv()
                    hop(part, h, side).start()

    def all_mates(buf, sem):
        there = buf.at[pl.ds(0, (CORES * K - 1) * POS)]
        return remote(there, there, sem.at[0], sem.at[1], (sibling, mp))

    def place(d, w):
        rows = pl.ds(pl.multiple_of(w * WIDE, WIDE), WIDE)
        cotangents = pl.ds(pl.multiple_of(d * R + w * WIDE, WIDE), WIDE)
        return d * 2 + w, pl.ds(d * HERE, HERE), rows, cotangents

    def score(d, w):
        i, docs, rows, _ = place(d, w)
        s = dot(kbuf[docs, :], qbuf[rows, :], ((1,), (1,))) * SCALE
        top = jnp.max(s, axis=0, keepdims=True)
        p = jnp.exp(s - top)
        total = jnp.sum(p, axis=0, keepdims=True)
        pbuf[i] = p
        p16[d, :, rows] = p.astype(BF16)
        mstat[d, :, rows] = top
        tstat[d, :, rows] = total
        logs[z, d, :, rows] = top + jnp.log(total)

    def weigh(d, w):
        i, docs, rows, cotangents = place(d, w)
        c = dot(vbuf[docs, :], gbuf[cotangents, :], ((1,), (1,)))
        wbuf[i] = c
        deltas[z, d, :, rows] = jnp.sum(pbuf[i] * c, axis=0, keepdims=True) / tstat[d, :, rows]

    def settle(d, w):
        i, _, rows, _ = place(d, w)
        s16[d, :, rows] = (pbuf[i] * (wbuf[i] - deltas[z, d, :, rows])).astype(BF16)

    late = lax.div(lax.rem(z, OWNERS), 2)
    early = 1 - late
    for copy in own[1:]:
        copy.wait()

    @pl.when(core == home)
    def _():
        own[0].wait()
        cotangent_share().wait_recv()

    all_mates(kbuf, ksem).wait_recv()
    for d in range(CORES):
        score(d, early)
    all_mates(vbuf, vsem).wait_recv()
    for d in range(CORES):
        weigh(d, early)
        settle(d, early)

    def last(part):
        @pl.when(core != home)
        def _():
            for side in range(2):
                arrival(part, 3, side).wait_recv()

    def tell(stat, sem):
        for d in (4, 3, 5, 2, 6, 1, 7):
            remote(stat.at[z], stat.at[z], sem.at[0], sem.at[1], ringmate(d)).start()

    def told(stat, sem):
        there = stat.at[pl.ds(0, Z - 1)]
        return remote(there, there, sem.at[0], sem.at[1], ringmate(1))

    last(0)
    for d in range(CORES):
        score(d, late)
    tell(logs, lsem)
    for d in range(CORES):
        last(1 + d)
        weigh(d, late)
    tell(deltas, dsem)
    for d in range(CORES):
        docs = pl.ds(d * HERE, HERE)
        settle(d, late)
        aq[d] = dot(s16[d], kbuf[docs, :], ((0,), (0,)))
        bq[d] = dot(p16[d], kbuf[docs, :], ((0,), (0,)))

    def columns(rows):
        return jnp.concatenate(rows + [jnp.zeros((8 - len(rows), R), F32)], axis=0).T

    def back(stage, out, sem, d, values):
        stage[d * HERE : (d + 1) * HERE, :] = values.astype(BF16)
        there = out.at[0, :, cols_of(k, core)]

        @pl.loop(0, K - 1)
        def _(e):
            j, to = far_mate(e)
            remote(stage.at[pos_of(j, d)], there, sem.at[0], sem.at[1], (first_core + d, to)).start()

        @pl.when(core != d)
        def _():
            remote(stage.at[pos_of(k, d)], there, sem.at[0], sem.at[1], (sibling, mp)).start()

    told(logs, lsem).wait_recv()
    weights, factors = [], []
    for d in range(CORES):
        parts = [logs[j, d] for j in range(Z)]
        peak = parts[0]
        for part in parts[1:]:
            peak = jnp.maximum(peak, part)
        shares = [jnp.exp(part - peak) for part in parts]
        whole = shares[0]
        for part in shares[1:]:
            whole = whole + part
        weights.append([share / whole for share in shares])
        factors.append(jnp.exp(mstat[d] - (peak + jnp.log(whole))))
    factor = columns(factors)

    def value_part(d):
        rows = gbuf[d * R : (d + 1) * R, :].astype(F32) * factor[:, d : d + 1]
        return dot(p16[d], rows.astype(BF16), ((1,), (0,)))

    back(dvst, dv_out, dvsem, 0, value_part(0))

    aq[0] = factor[:, 0:1] * aq[0] + factor[:, 1:2] * aq[1]

    told(deltas, dsem).wait_recv()
    changes = []
    for d in range(CORES):
        delta = weights[d][0] * deltas[0, d]
        for j in range(1, Z):
            delta = delta + weights[d][j] * deltas[j, d]
        changes.append(factors[d] * (deltas[z, d] - delta))
    change = columns(changes)

    def z_copy(b, c):
        src = zsend.at[b, pl.ds(c * HALF, HALF)]
        where = (first_core + c, k * Z + core * OWNERS + b)
        return remote(src, zrecv.at[z], zsem.at[0], zsem.at[1], where)

    def z_own():
        src = zsend.at[lax.rem(z, OWNERS), pl.ds(pl.multiple_of((1 - core) * HALF, HALF), HALF)]
        return remote(src, zrecv.at[z], zown.at[0], zown.at[1], (sibling, mp))

    for b in range(OWNERS):
        rows = slice(b * BLOCK, (b + 1) * BLOCK)
        part = aq[0, rows, :] + change[rows, 0:1] * bq[0, rows, :] + change[rows, 1:2] * bq[1, rows, :]
        zsend[b] = (part * SCALE).astype(BF16)

        @pl.when(core * OWNERS + b != z)
        def _(b=b):
            for c in range(CORES):
                z_copy(b, c).start()

    @pl.when(core == home)
    def _():
        z_own().start()
        mine = pl.ds(pl.multiple_of(core * HALF, HALF), HALF)
        zrecv[z] = zsend[lax.rem(z, OWNERS), mine, :]

    def key_part(d):
        rows = qbuf[...].astype(F32)
        main = (rows * (factor[:, d : d + 1] * SCALE)).astype(BF16)
        rest = (rows * (change[:, d : d + 1] * SCALE)).astype(BF16)
        return dot(s16[d], main, ((1,), (0,))) + dot(p16[d], rest, ((1,), (0,)))

    back(dvst, dv_out, dvsem, 1, value_part(1))
    for d in range(CORES):
        back(dkst, dk_out, dksem, d, key_part(d))
    kept = [
        pltpu.make_async_copy(dvst.at[pos_of(k, core)], dv_out.at[0, :, cols_of(k, core)], own_sem.at[0]),
        pltpu.make_async_copy(dkst.at[pos_of(k, core)], dk_out.at[0, :, cols_of(k, core)], own_sem.at[1]),
    ]
    for copy in kept:
        copy.start()

    @pl.when(core == home)
    def _():
        for side in range(2):
            hop(0, 0, side).wait_send()

    for side in range(2):
        cotangent_hop(side).wait_send()

    @pl.when(core != home)
    def _():
        cotangent_share().wait_send()

    for h in range(1, 4):
        for side in range(2):

            @pl.when(concerns(h - 1, side))
            def _(h=h, side=side):
                for part in range(3):
                    hop(part, h, side).wait_send()

    all_mates(kbuf, ksem).wait_send()
    all_mates(vbuf, vsem).wait_send()
    told(logs, lsem).wait_send()
    told(deltas, dsem).wait_send()

    @pl.when(core != home)
    def _():
        z_own().wait_recv()

    pieces = zrecv.at[pl.ds(0, Z - 1)]
    remote(pieces, pieces, zsem.at[0], zsem.at[1], ringmate(1)).wait_recv()
    half_sum = zrecv[0].astype(F32)
    for j in range(1, Z):
        half_sum = half_sum + zrecv[j].astype(F32)
    yrecv[dp] = half_sum.astype(BF16)

    for d in range(1, DOCS):
        remote(yrecv.at[dp], yrecv.at[dp], ysem.at[0], ysem.at[1], doc(d)).start()

    def all_docs():
        there = yrecv.at[pl.ds(0, DOCS - 1)]
        return remote(there, there, ysem.at[0], ysem.at[1], doc(1))

    all_docs().wait_recv()
    for copy in kept:
        copy.wait()
    for out, sem in ((dv_out, dvsem), (dk_out, dksem)):
        there = out.at[0, :, pl.ds(0, (CORES * K - 1) * DH)]
        done = remote(there, there, sem.at[0], sem.at[1], (sibling, mp))
        done.wait_send()
        done.wait_recv()

    @pl.when(core == home)
    def _():
        z_own().wait_send()

    for b in range(OWNERS):

        @pl.when(core * OWNERS + b != z)
        def _(b=b):
            for c in range(CORES):
                z_copy(b, c).wait_send()

    all_docs().wait_send()


def finish(parts, dk_in, dv_in, dq_out, dk_out, dv_out, total, sem):
    copies = [
        pltpu.make_async_copy(dk_in, dk_out, sem.at[0]),
        pltpu.make_async_copy(dv_in, dv_out, sem.at[1]),
    ]
    for copy in copies:
        copy.start()
    for h in range(2):
        total[pl.ds(h * HALF, HALF), :] = parts[h].astype(F32) + parts[2 + h].astype(F32)
    copies.append(pltpu.make_async_copy(total, dq_out, sem.at[2]))
    copies[2].start()
    for copy in copies:
        copy.wait()


def on_device(queries, keys, values, out_cotangent):
    queries, keys, values, out_cotangent = (
        pltpu.with_memory_space_constraint(x, pltpu.HBM) for x in (queries, keys, values, out_cotangent)
    )
    anywhere = pl.BlockSpec(memory_space=pl.ANY)
    inside = pl.BlockSpec(memory_space=pltpu.VMEM)
    dma = pltpu.SemaphoreType.DMA
    parts, key_gradient, value_gradient = pl.pallas_call(
        kernel,
        out_shape=(
            pltpu.VMEM((DOCS, HALF, DH), BF16),
            pltpu.VMEM(keys.shape, BF16),
            pltpu.VMEM(values.shape, BF16),
        ),
        in_specs=[anywhere] * 4,
        out_specs=[inside] * 3,
        scratch_shapes=[
            pltpu.VMEM((POS, HEADS * DH), BF16),
            pltpu.VMEM((POS, HEADS * DH), BF16),
            pltpu.VMEM((BLOCK, DH), BF16),
            pltpu.VMEM((CORES * HERE, DH), BF16),
            pltpu.VMEM((CORES * HERE, DH), BF16),
            pltpu.VMEM((R, DH), BF16),
            pltpu.VMEM((CORES * R, DH), BF16),
            pltpu.VMEM((2 * CORES, HERE, WIDE), F32),
            pltpu.VMEM((2 * CORES, HERE, WIDE), F32),
            pltpu.VMEM((CORES, HERE, R), BF16),
            pltpu.VMEM((CORES, HERE, R), BF16),
            pltpu.VMEM((CORES, R, DH), F32),
            pltpu.VMEM((CORES, R, DH), F32),
            pltpu.VMEM((CORES * HERE, DH), BF16),
            pltpu.VMEM((CORES * HERE, DH), BF16),
            pltpu.VMEM((OWNERS, BLOCK, DH), BF16),
            pltpu.VMEM((Z, HALF, DH), BF16),
            pltpu.VMEM((CORES, 1, R), F32),
            pltpu.VMEM((CORES, 1, R), F32),
            pltpu.VMEM((Z, CORES, 1, R), F32),
            pltpu.VMEM((Z, CORES, 1, R), F32),
            dma((4,)), dma((2,)), dma((2,)), dma((24,)), dma((24,)), dma((4,)), dma((2,)), dma((2,)),
            dma((2,)), dma((2,)), dma((2,)), dma((2,)), dma((2,)),
        ],
        compiler_params=pltpu.CompilerParams(
            collective_id=0, has_side_effects=True, vmem_limit_bytes=48 * 2**20
        ),
        cost_estimate=pl.CostEstimate(
            flops=10 * HERE * CORES * R * DH, bytes_accessed=4 * 2**20, transcendentals=HERE * CORES * R
        ),
    )(queries, keys, values, out_cotangent)
    return pl.pallas_call(
        finish,
        out_shape=(
            jax.ShapeDtypeStruct((BLOCK, DH), F32),
            jax.ShapeDtypeStruct(keys.shape, BF16),
            jax.ShapeDtypeStruct(values.shape, BF16),
        ),
        in_specs=[inside] * 3,
        out_specs=[anywhere] * 3,
        scratch_shapes=[pltpu.VMEM((BLOCK, DH), F32), dma((3,))],
        compiler_params=pltpu.CompilerParams(vmem_limit_bytes=4 * 2**20),
    )(parts, key_gradient, value_gradient)


def solution(mesh):
    placed = (P("mp", None), P("dp", "mp", None), P("dp", "mp", None), P("dp", "mp", None))
    return jax.shard_map(
        on_device,
        mesh=mesh,
        in_specs=placed,
        out_specs=(P("mp", None), P("dp", "mp", None), P("dp", "mp", None)),
        check_vma=False,
    )
```

```python
import math

import jax
import jax.numpy as jnp
from jax import lax
from jax.experimental import pallas as pl
from jax.experimental.pallas import tpu as pltpu
from jax.sharding import PartitionSpec as P

HEADS = 16
DH = 256
R = 768
DOCS = 4
MP = 64
CORES = 2
Z = 8
OWNERS = Z // 2
K = MP // Z
BLOCK = 192
HALF = BLOCK // 2
POS = 64
HERE = K * POS
WIDE = 2 * BLOCK
SCALE = 1.0 / math.sqrt(DH)
MESH = pl.DeviceIdType.MESH
F32 = jnp.float32
BF16 = jnp.bfloat16


def dot(a, b, dims):
    return lax.dot_general(a, b, (dims, ((), ())), preferred_element_type=F32)


def kernel(
    q_in, k_in, v_in, g_in,
    yrecv, dk_out, dv_out,
    kown, vown, gown, kbuf, vbuf, qbuf, gbuf, pbuf, wbuf, sp16, aq, bq, dkst, dvst,
    zsend, zrecv, mstat, tstat, logs, deltas,
    own_sem, ksem, vsem, rsend, rrecv, gsem, lsem, dsem, dksem, dvsem, zsem, zown, ysem,
):
    dp, mp = lax.axis_index("dp"), lax.axis_index("mp")
    k, z = lax.div(mp, Z), lax.rem(mp, Z)
    core = lax.rem(dp, CORES)
    first_core = dp - core
    sibling = first_core + 1 - core
    home = lax.div(z, OWNERS)
    right = k * Z + lax.rem(z + 1, Z)
    left = k * Z + lax.rem(z + Z - 1, Z)

    def remote(src, dst, ssem, rsem, where):
        return pltpu.make_async_remote_copy(
            src_ref=src, dst_ref=dst, send_sem=ssem, recv_sem=rsem, device_id=where, device_id_type=MESH
        )

    def mate(d):
        j = lax.rem(k + d, K)
        return j, j * Z + z

    def far_mate(e):
        i, x, y = lax.rem(e, 4), lax.div(k, 2), lax.rem(k, 2)
        dx = 2 + 3 * i + 3 * lax.div(i, 2) + 2 * lax.div(i, 3)
        j = lax.rem(x + dx, 4) * 2 + lax.rem(y + 1 - lax.div(e, 4), 2)
        return j, j * Z + z

    def ringmate(d):
        return dp, k * Z + lax.rem(z + d, Z)

    def doc(d):
        return lax.rem(dp + d, DOCS), mp

    barrier = pltpu.get_barrier_semaphore()
    partners = [(first_core + c, mate(d)[1]) for d in range(1, K) for c in range(CORES)]
    partners += [(sibling, right), (sibling, left)]
    partners += [ringmate(d) for d in range(1, Z)]
    partners += [doc(d) for d in range(1, DOCS)]
    for where in partners:
        pl.semaphore_signal(barrier, inc=1, device_id=where, device_id_type=MESH)

    def pos_of(j, which=0):
        return pl.ds(pl.multiple_of(which * HERE + j * POS, POS), POS)

    def cols_of(j, which):
        return pl.ds(pl.multiple_of((j * CORES + which) * DH, DH), DH)

    def piece(part, j, h, side):
        start = lax.rem(j, OWNERS) * BLOCK + (side * HALF if h == 3 else 0)
        size = HALF if h == 3 else BLOCK
        if part == 0:
            return qbuf.at[pl.ds(pl.multiple_of(start, 32), size)]
        return gbuf.at[pl.ds(pl.multiple_of((part - 1) * R + start, 32), size)]

    def own_queries():
        return qbuf.at[pl.ds(pl.multiple_of(lax.rem(z, OWNERS) * BLOCK, 32), BLOCK)]

    def own_cotangent():
        return gbuf.at[pl.ds(pl.multiple_of(core * R + lax.rem(z, OWNERS) * BLOCK, 32), BLOCK)]

    def slot(part, h, side):
        return (part * 2 + side) * 4 + h

    def hop(part, h, side):
        j = lax.rem(z + (Z - h if side == 0 else h), Z)
        there = piece(part, j, h, side)
        src = own_queries() if h == 0 else there
        i = slot(part, h, side)
        return remote(src, there, rsend.at[i], rrecv.at[i], (dp, right if side == 0 else left))

    def arrival(part, h, side):
        j = lax.rem(z + (Z - 1 - h if side == 0 else h + 1), Z)
        there = piece(part, j, h, side)
        i = slot(part, h, side)
        return remote(there, there, rsend.at[i], rrecv.at[i], (dp, right if side == 0 else left))

    def concerns(h, side):
        j = lax.rem(z + (Z - 1 - h if side == 0 else h + 1), Z)
        return lax.div(j, OWNERS) == core

    def cotangent_hop(side):
        where = (first_core + home, right if side == 0 else left)
        return remote(gown, own_cotangent(), gsem.at[side], rrecv.at[4 * side + 8 + 8 * core], where)

    def cotangent_share():
        return remote(gown, own_cotangent(), gsem.at[2], gsem.at[3], (sibling, mp))

    staged = [
        pltpu.make_async_copy(q_in, own_queries(), own_sem.at[0]),
        pltpu.make_async_copy(g_in.at[0], gown, own_sem.at[1]),
        pltpu.make_async_copy(k_in.at[0], kown, own_sem.at[2]),
        pltpu.make_async_copy(v_in.at[0], vown, own_sem.at[3]),
    ]
    own = [
        pltpu.make_async_copy(gown, own_cotangent(), own_sem.at[1]),
        pltpu.make_async_copy(kown.at[:, cols_of(k, core)], kbuf.at[pos_of(k, core)], own_sem.at[2]),
        pltpu.make_async_copy(vown.at[:, cols_of(k, core)], vbuf.at[pos_of(k, core)], own_sem.at[3]),
    ]

    for copy in staged[1:]:
        copy.start()

    @pl.when(core == home)
    def _():
        staged[0].start()
        staged[0].wait()

    for copy in staged[1:]:
        copy.wait()
    pl.semaphore_wait(barrier, len(partners))

    @pl.when(core == home)
    def _():
        for side in range(2):
            hop(0, 0, side).start()

    for side in range(2):
        cotangent_hop(side).start()

    @pl.when(core != home)
    def _():
        cotangent_share().start()

    def spread(src, buf, sem):
        @pl.loop(0, K - 1)
        def _(e):
            j, there = far_mate(e)
            for c in range(CORES):
                where = (first_core + c, there)
                remote(src.at[:, cols_of(j, c)], buf.at[pos_of(k, core)], sem.at[0], sem.at[1], where).start()


        where = (sibling, mp)
        remote(src.at[:, cols_of(k, 1 - core)], buf.at[pos_of(k, core)], sem.at[0], sem.at[1], where).start()

    spread(kown, kbuf, ksem)
    for copy in own[1:]:
        copy.start()

    @pl.when(core == home)
    def _():
        own[0].start()


    for h in range(1, 4):
        if h == 2:
            spread(vown, vbuf, vsem)
        for part in range(3):
            for side in range(2):

                @pl.when(concerns(h - 1, side))
                def _(h=h, part=part, side=side):
                    arrival(part, h - 1, side).wait_recv()
                    hop(part, h, side).start()

    def all_mates(buf, sem):
        there = buf.at[pl.ds(0, (CORES * K - 1) * POS)]
        return remote(there, there, sem.at[0], sem.at[1], (sibling, mp))

    def place(d, w):
        rows = pl.ds(pl.multiple_of(w * WIDE, WIDE), WIDE)
        cotangents = pl.ds(pl.multiple_of(d * R + w * WIDE, WIDE), WIDE)
        return d * 2 + w, pl.ds(d * HERE, HERE), rows, cotangents

    def score(d, w):
        i, docs, rows, _ = place(d, w)
        s = dot(kbuf[docs, :], qbuf[rows, :], ((1,), (1,))) * SCALE
        top = jnp.max(s, axis=0, keepdims=True)
        p = jnp.exp(s - top)
        total = jnp.sum(p, axis=0, keepdims=True)
        pbuf[i] = p
        sp16[d, :, pl.ds(pl.multiple_of(R + w * WIDE, WIDE), WIDE)] = p.astype(BF16)
        mstat[d, :, rows] = top
        tstat[d, :, rows] = total
        logs[z, d, :, rows] = top + jnp.log(total)

    def weigh(d, w):
        i, docs, rows, cotangents = place(d, w)
        c = dot(vbuf[docs, :], gbuf[cotangents, :], ((1,), (1,)))
        wbuf[i] = c
        deltas[z, d, :, rows] = jnp.sum(pbuf[i] * c, axis=0, keepdims=True) / tstat[d, :, rows]

    def settle(d, w):
        i, _, rows, _ = place(d, w)
        sp16[d, :, rows] = (pbuf[i] * (wbuf[i] - deltas[z, d, :, rows])).astype(BF16)

    late = lax.div(lax.rem(z, OWNERS), 2)
    early = 1 - late
    for copy in own[1:]:
        copy.wait()

    @pl.when(core == home)
    def _():
        own[0].wait()
        cotangent_share().wait_recv()

    all_mates(kbuf, ksem).wait_recv()
    for d in range(CORES):
        score(d, early)
    all_mates(vbuf, vsem).wait_recv()
    for d in range(CORES):
        weigh(d, early)
        settle(d, early)

    def last(part):
        @pl.when(core != home)
        def _():
            for side in range(2):
                arrival(part, 3, side).wait_recv()

    def tell(stat, sem):
        for d in (4, 3, 5, 2, 6, 1, 7):
            remote(stat.at[z], stat.at[z], sem.at[0], sem.at[1], ringmate(d)).start()

    def told(stat, sem):
        there = stat.at[pl.ds(0, Z - 1)]
        return remote(there, there, sem.at[0], sem.at[1], ringmate(1))

    last(0)
    for d in range(CORES):
        score(d, late)
    tell(logs, lsem)
    for d in range(CORES):
        last(1 + d)
        weigh(d, late)
    tell(deltas, dsem)
    for d in range(CORES):
        docs = pl.ds(d * HERE, HERE)
        settle(d, late)
        aq[d] = dot(sp16[d, :, :R], kbuf[docs, :], ((0,), (0,)))
        bq[d] = dot(sp16[d, :, R:], kbuf[docs, :], ((0,), (0,)))

    def columns(rows):
        return jnp.concatenate(rows + [jnp.zeros((8 - len(rows), R), F32)], axis=0).T

    def back(stage, out, sem, d, values):
        stage[d * HERE : (d + 1) * HERE, :] = values.astype(BF16)
        there = out.at[0, :, cols_of(k, core)]

        @pl.loop(0, K - 1)
        def _(e):
            j, to = far_mate(e)
            remote(stage.at[pos_of(j, d)], there, sem.at[0], sem.at[1], (first_core + d, to)).start()

        @pl.when(core != d)
        def _():
            remote(stage.at[pos_of(k, d)], there, sem.at[0], sem.at[1], (sibling, mp)).start()

    told(logs, lsem).wait_recv()
    weights, factors = [], []
    for d in range(CORES):
        parts = [logs[j, d] for j in range(Z)]
        peak = parts[0]
        for part in parts[1:]:
            peak = jnp.maximum(peak, part)
        shares = [jnp.exp(part - peak) for part in parts]
        whole = shares[0]
        for part in shares[1:]:
            whole = whole + part
        weights.append([share / whole for share in shares])
        factors.append(jnp.exp(mstat[d] - (peak + jnp.log(whole))))
    factor = columns(factors)

    def value_part(d):
        rows = gbuf[d * R : (d + 1) * R, :].astype(F32) * factor[:, d : d + 1]
        return dot(sp16[d, :, R:], rows.astype(BF16), ((1,), (0,)))

    back(dvst, dv_out, dvsem, 0, value_part(0))

    aq[0] = factor[:, 0:1] * aq[0] + factor[:, 1:2] * aq[1]

    told(deltas, dsem).wait_recv()
    changes = []
    for d in range(CORES):
        delta = weights[d][0] * deltas[0, d]
        for j in range(1, Z):
            delta = delta + weights[d][j] * deltas[j, d]
        changes.append(factors[d] * (deltas[z, d] - delta))
    change = columns(changes)

    def z_copy(b, c):
        src = zsend.at[b, pl.ds(pl.multiple_of(c * HALF, 32), HALF)]
        where = (first_core + c, k * Z + core * OWNERS + b)
        return remote(src, zrecv.at[z], zsem.at[0], zsem.at[1], where)

    def z_own():
        src = zsend.at[lax.rem(z, OWNERS), pl.ds(pl.multiple_of((1 - core) * HALF, HALF), HALF)]
        return remote(src, zrecv.at[z], zown.at[0], zown.at[1], (sibling, mp))

    for b in range(OWNERS):
        rows = slice(b * BLOCK, (b + 1) * BLOCK)
        part = aq[0, rows, :] + change[rows, 0:1] * bq[0, rows, :] + change[rows, 1:2] * bq[1, rows, :]
        zsend[b] = (part * SCALE).astype(BF16)

        @pl.when(core * OWNERS + b != z)
        def _(b=b):
            for other in range(CORES):
                z_copy(b, lax.rem(core + 1 + other, CORES)).start()

    @pl.when(core == home)
    def _():
        z_own().start()
        mine = pl.ds(pl.multiple_of(core * HALF, HALF), HALF)
        zrecv[z] = zsend[lax.rem(z, OWNERS), mine, :]

    def key_part(d):
        rows = qbuf[...].astype(F32)
        main = (rows * (factor[:, d : d + 1] * SCALE)).astype(BF16)
        rest = (rows * (change[:, d : d + 1] * SCALE)).astype(BF16)
        return dot(sp16[d], jnp.concatenate([main, rest], axis=0), ((1,), (0,)))

    back(dvst, dv_out, dvsem, 1, value_part(1))
    for d in range(CORES):
        back(dkst, dk_out, dksem, d, key_part(d))
    kept = [
        pltpu.make_async_copy(dvst.at[pos_of(k, core)], dv_out.at[0, :, cols_of(k, core)], own_sem.at[0]),
        pltpu.make_async_copy(dkst.at[pos_of(k, core)], dk_out.at[0, :, cols_of(k, core)], own_sem.at[1]),
    ]
    for copy in kept:
        copy.start()

    @pl.when(core == home)
    def _():
        for side in range(2):
            hop(0, 0, side).wait_send()

    for side in range(2):
        cotangent_hop(side).wait_send()

    @pl.when(core != home)
    def _():
        cotangent_share().wait_send()

    for h in range(1, 4):
        for side in range(2):

            @pl.when(concerns(h - 1, side))
            def _(h=h, side=side):
                for part in range(3):
                    hop(part, h, side).wait_send()

    all_mates(kbuf, ksem).wait_send()
    all_mates(vbuf, vsem).wait_send()
    told(logs, lsem).wait_send()
    told(deltas, dsem).wait_send()

    @pl.when(core != home)
    def _():
        z_own().wait_recv()

    pieces = zrecv.at[pl.ds(0, Z - 1)]
    remote(pieces, pieces, zsem.at[0], zsem.at[1], ringmate(1)).wait_recv()
    half_sum = zrecv[0].astype(F32)
    for j in range(1, Z):
        half_sum = half_sum + zrecv[j].astype(F32)
    yrecv[dp] = half_sum.astype(BF16)

    for d in range(1, DOCS):
        remote(yrecv.at[dp], yrecv.at[dp], ysem.at[0], ysem.at[1], doc(d)).start()

    def all_docs():
        there = yrecv.at[pl.ds(0, DOCS - 1)]
        return remote(there, there, ysem.at[0], ysem.at[1], doc(1))

    all_docs().wait_recv()
    for copy in kept:
        copy.wait()
    for out, sem in ((dv_out, dvsem), (dk_out, dksem)):
        there = out.at[0, :, pl.ds(0, (CORES * K - 1) * DH)]
        done = remote(there, there, sem.at[0], sem.at[1], (sibling, mp))
        done.wait_send()
        done.wait_recv()

    @pl.when(core == home)
    def _():
        z_own().wait_send()

    for b in range(OWNERS):

        @pl.when(core * OWNERS + b != z)
        def _(b=b):
            for c in range(CORES):
                z_copy(b, c).wait_send()

    all_docs().wait_send()


def finish(parts, dk_in, dv_in, dq_out, dk_out, dv_out, total, sem):
    copies = [
        pltpu.make_async_copy(dk_in, dk_out, sem.at[0]),
        pltpu.make_async_copy(dv_in, dv_out, sem.at[1]),
    ]
    for copy in copies:
        copy.start()
    for h in range(2):
        total[pl.ds(h * HALF, HALF), :] = parts[h].astype(F32) + parts[2 + h].astype(F32)
    copies.append(pltpu.make_async_copy(total, dq_out, sem.at[2]))
    copies[2].start()
    for copy in copies:
        copy.wait()


def on_device(queries, keys, values, out_cotangent):
    queries, keys, values, out_cotangent = (
        pltpu.with_memory_space_constraint(x, pltpu.HBM) for x in (queries, keys, values, out_cotangent)
    )
    anywhere = pl.BlockSpec(memory_space=pl.ANY)
    inside = pl.BlockSpec(memory_space=pltpu.VMEM)
    dma = pltpu.SemaphoreType.DMA
    parts, key_gradient, value_gradient = pl.pallas_call(
        kernel,
        out_shape=(
            pltpu.VMEM((DOCS, HALF, DH), BF16),
            pltpu.VMEM(keys.shape, BF16),
            pltpu.VMEM(values.shape, BF16),
        ),
        in_specs=[anywhere] * 4,
        out_specs=[inside] * 3,
        scratch_shapes=[
            pltpu.VMEM((POS, HEADS * DH), BF16),
            pltpu.VMEM((POS, HEADS * DH), BF16),
            pltpu.VMEM((BLOCK, DH), BF16),
            pltpu.VMEM((CORES * HERE, DH), BF16),
            pltpu.VMEM((CORES * HERE, DH), BF16),
            pltpu.VMEM((R, DH), BF16),
            pltpu.VMEM((CORES * R, DH), BF16),
            pltpu.VMEM((2 * CORES, HERE, WIDE), F32),
            pltpu.VMEM((2 * CORES, HERE, WIDE), F32),
            pltpu.VMEM((CORES, HERE, 2 * R), BF16),
            pltpu.VMEM((CORES, R, DH), F32),
            pltpu.VMEM((CORES, R, DH), F32),
            pltpu.VMEM((CORES * HERE, DH), BF16),
            pltpu.VMEM((CORES * HERE, DH), BF16),
            pltpu.VMEM((OWNERS, BLOCK, DH), BF16),
            pltpu.VMEM((Z, HALF, DH), BF16),
            pltpu.VMEM((CORES, 1, R), F32),
            pltpu.VMEM((CORES, 1, R), F32),
            pltpu.VMEM((Z, CORES, 1, R), F32),
            pltpu.VMEM((Z, CORES, 1, R), F32),
            dma((4,)), dma((2,)), dma((2,)), dma((24,)), dma((24,)), dma((4,)), dma((2,)), dma((2,)),
            dma((2,)), dma((2,)), dma((2,)), dma((2,)), dma((2,)),
        ],
        compiler_params=pltpu.CompilerParams(
            collective_id=0, has_side_effects=True, vmem_limit_bytes=48 * 2**20
        ),
        cost_estimate=pl.CostEstimate(
            flops=10 * HERE * CORES * R * DH, bytes_accessed=4 * 2**20, transcendentals=HERE * CORES * R
        ),
    )(queries, keys, values, out_cotangent)
    return pl.pallas_call(
        finish,
        out_shape=(
            jax.ShapeDtypeStruct((BLOCK, DH), F32),
            jax.ShapeDtypeStruct(keys.shape, BF16),
            jax.ShapeDtypeStruct(values.shape, BF16),
        ),
        in_specs=[inside] * 3,
        out_specs=[anywhere] * 3,
        scratch_shapes=[pltpu.VMEM((BLOCK, DH), F32), dma((3,))],
        compiler_params=pltpu.CompilerParams(vmem_limit_bytes=4 * 2**20),
    )(parts, key_gradient, value_gradient)


def solution(mesh):
    placed = (P("mp", None), P("dp", "mp", None), P("dp", "mp", None), P("dp", "mp", None))
    return jax.shard_map(
        on_device,
        mesh=mesh,
        in_specs=placed,
        out_specs=(P("mp", None), P("dp", "mp", None), P("dp", "mp", None)),
        check_vma=False,
    )
```
